32 devices in a mesh: tm: 8 (over z, core), ang: 2 (over x), ax: 2 (over y).
Axes of the slice: x: 2, y: 2, z: 4, core: 2. Of those that a mesh axis runs over, the one named last changes fastest.
Arguments:
- window_starts: float32 [8, 32, 32, 1152], P('tm', 'ang', 'ax'), may hold values from -6 to 6
- drive_source: float32 [8, 32, 32, 1152], P('tm', 'ang', 'ax'), may hold values from -6 to 6
- region_ids: int32 [32, 32, 1152], P('ang', 'ax'), may hold values from 0 to 7
- window_steps: int32 [8], replicated, may hold values from 1 to 4, as said below
- reluctivity: float32 [8], replicated, may hold values from 0.3 to 1
- resistivity: float32 [8], replicated, may hold values from 0.3 to 1
- relax_rates: float32 [8], replicated, may hold values from 0.02 to 0.14
Outputs:
- new_starts: float32 [8, 32, 32, 1152], P('tm', 'ang', 'ax')
The draws below stay inside these ranges and needn't reach their ends.
Inputs may be any that keep to these rules, and one draw needn't show every extreme that they name: `window_steps`: every window takes 1 to 4 fine steps, and some window takes 4.
All inputs are finite; a program needn't handle non-finite values.
Results may differ from the reference program's by a relative error of at most 0.0003.
Values sent between devices are 32-bit elements; how exact they have to be, the bound alone decides.
A program may use at most 128 MiB of HBM per device.

```python
import math
import jax
import jax.numpy as jnp
from jax import lax

RAD = 1152
STEPS = 4
REGIONS = 8
TW = 8
NA = 32
NZ = 32


def draw_window_steps(key, part):
    first_key, second_key = jax.random.split(jax.random.fold_in(key, 17))
    counts = jax.random.randint(first_key, (TW,), 1, STEPS + 1)
    place = jax.random.randint(second_key, (), 0, TW)
    return jnp.where(jnp.arange(TW) == place, STEPS, counts).astype(jnp.int32)


def plant(values, stream_key, smallest, top_value):
    spot = [jax.random.randint(jax.random.fold_in(stream_key, axis), (), 0, length) for axis, length in enumerate(values.shape)]
    widest = values.shape.index(max(values.shape))
    beside = spot[:widest] + [(spot[widest] + 1) % values.shape[widest]] + spot[widest + 1:]
    return values.at[tuple(spot)].set(smallest).at[tuple(beside)].set(top_value)


def block_scale(rng, shape, cuts, smallest, largest):
    def one(dim, shards_of):
        heights = jax.random.uniform(jax.random.fold_in(jax.random.fold_in(rng, 6), dim), (shards_of,), jnp.float32, smallest / len(cuts), largest / len(cuts))
        return jnp.repeat(jnp.exp(heights), shape[dim] // shards_of).reshape((-1,) + (1,) * (len(shape) - dim - 1))

    loudness = one(*cuts[0])
    for cut in cuts[1:]:
        loudness = loudness * one(*cut)
    return loudness


def centred(rng, extent, scale, reach, shards=(), kind=jnp.bfloat16):
    gain = block_scale(rng, extent, shards, -0.22, 0.18) if shards else 1.0
    values = jax.random.normal(rng, extent, jnp.float32) * scale * gain
    return jnp.minimum(jnp.maximum(values, -reach), reach).astype(kind)


def setup_inputs(seed: int = 0) -> dict:
    keys = jax.random.split(jax.random.key(seed), 8)
    window_starts = centred(keys[0], (TW, NA, NZ, RAD), 1.0, 6.0, ((0, 8), (1, 2), (2, 2)), jnp.float32)
    drive_source = centred(keys[1], (TW, NA, NZ, RAD), 1.0, 6.0, ((0, 8), (1, 2), (2, 2)), jnp.float32)
    region_ids = plant(jax.random.randint(keys[2], (NA, NZ, RAD), 0, REGIONS), jax.random.fold_in(keys[2], 1), 0, REGIONS - 1).astype(jnp.int32)
    window_steps = draw_window_steps(jax.random.fold_in(keys[7], 71), 0)
    reluctivity = jnp.clip(jax.random.uniform(keys[4], (REGIONS,), jnp.float32, 0.3, 1.0), 0.3, 1.0)
    resistivity = jnp.clip(jax.random.uniform(keys[5], (REGIONS,), jnp.float32, 0.3, 1.0), 0.3, 1.0)
    relax_rates = jnp.clip(jnp.exp(jax.random.uniform(keys[6], (REGIONS,), jnp.float32, math.log(0.02), math.log(0.14))), 0.02, 0.14)
    return dict(window_starts=window_starts, drive_source=drive_source, region_ids=region_ids, window_steps=window_steps, reluctivity=reluctivity, resistivity=resistivity, relax_rates=relax_rates)


radial_weight = 1.0
explicit_limit = 0.23

def lookup(region_ids, table):
    total = jnp.zeros(region_ids.shape, table.dtype)
    for region in range(table.shape[0]):
        total = total + jnp.where(region_ids == region, table[region], 0.0)
    return total

def radial_inverse(size):
    index = jnp.arange(size, dtype=jnp.float32)
    scale = jnp.sqrt(2.0 / (size + 1.0))
    basis = scale * jnp.sin(jnp.pi * (index[:, None] + 1.0) * (index[None, :] + 1.0) / (size + 1.0))
    eigen = 2.0 - 2.0 * jnp.cos(jnp.pi * (index + 1.0) / (size + 1.0))
    weighted = basis * (1.0 / (1.0 + radial_weight * eigen))[None, :]
    return jnp.dot(weighted, basis, precision=lax.Precision.HIGHEST, preferred_element_type=jnp.float32)

def restrict_pairs(field):
    return (field[0::2] + field[1::2]) * 0.5

def prolong_pairs(coarse):
    return jnp.repeat(coarse, 2, axis=0)

def fine_step(field, forcing, coupling, relax, inverse):
    axial = jnp.pad(field, ((0, 0), (1, 1), (0, 0)))
    beside = jnp.roll(field, 1, 0) + jnp.roll(field, -1, 0) + axial[:, 2:] + axial[:, :-2]
    moved = field + coupling * (beside - 4.0 * field) + relax * (forcing - field)
    shape = moved.shape
    flat = jnp.dot(moved.reshape(-1, shape[-1]), inverse, precision=lax.Precision.HIGHEST, preferred_element_type=jnp.float32)
    return flat.reshape(shape)

def reference(window_starts, drive_source, region_ids, window_steps, reluctivity, resistivity, relax_rates):
    coupling = explicit_limit * lookup(region_ids, reluctivity) * lookup(region_ids, resistivity)
    relax = lookup(region_ids, relax_rates)
    relax_coarse = restrict_pairs(relax)
    inverse = radial_inverse(window_starts.shape[-1])

    def window_terms(index):
        start = window_starts[index]
        forcing = drive_source[index]
        count = window_steps[index]
        field = start
        for turn in range(STEPS):
            field = jnp.where(turn < count, fine_step(field, forcing, coupling, relax, inverse), field)
        step_count = count.astype(relax_coarse.dtype)
        factor = 1.0 / (1.0 + step_count * relax_coarse)
        settled = step_count * relax_coarse * restrict_pairs(forcing) * factor
        change = field - prolong_pairs(restrict_pairs(start) * factor + settled)
        offset = settled + restrict_pairs(change)
        return (factor, offset, change)
    factors, offsets, changes = lax.map(window_terms, jnp.arange(TW, dtype=jnp.int32))

    def compose(carry, item):
        return ((carry[0] * item[0], item[0] * carry[1] + item[1]), None)
    ones = jnp.ones_like(relax_coarse)
    (total_factor, total_offset), unused = lax.scan(compose, (ones, jnp.zeros_like(relax_coarse)), (factors, offsets))
    first = total_offset / (1.0 - total_factor)

    def advance(state, item):
        return (item[0] * state + item[1], state)
    last, coarse = lax.scan(advance, first, (factors, offsets))
    previous = jnp.roll(changes, 1, axis=0)
    return jax.vmap(prolong_pairs)(coarse - jax.vmap(restrict_pairs)(previous)) + previous
```

```python
import functools

import jax
import jax.numpy as jnp
import ml_dtypes
import numpy as np
from jax import lax
from jax.experimental import pallas as pl
from jax.experimental.pallas import tpu as pltpu
from jax.sharding import PartitionSpec as P

STEPS = 4
LANES = 384
WIDE = 256
EDGE = 128
CHUNK = 128
TALL = 8
SPLIT = 2
VMEM_LIMIT = 60 * 2**20
AHEAD = 5
LAG = 5
GROUPS = (1, 2, 3, 4)

radial_weight = 1.0
explicit_limit = 0.23
F32 = jnp.float32
BF16 = jnp.bfloat16


def inverse_blocks(size):
    middle = 2.0 + 1.0 / radial_weight
    r = (middle - np.sqrt(middle * middle - 4.0)) / 2.0
    index = np.arange(size, dtype=np.float64)
    low = np.minimum(index[:, None], index[None, :])
    high = np.maximum(index[:, None], index[None, :])
    full = r ** (high - low) * (1 - r ** (2 * low + 2)) * (1 - r ** (2 * (size - high)))
    full = full / ((1 / r - r) * (1 - r ** (2 * size + 2)) * radial_weight)
    full = full.astype(np.float32)
    blocks, places, seen = [], [], {}
    for start in range(0, size, WIDE):
        stop = min(start + WIDE, size)
        first, last = max(start - EDGE, 0), min(stop + EDGE, size)
        block = np.ascontiguousarray(full[first:last, start:stop])
        key = (block.shape, block.tobytes())
        if key not in seen:
            seen[key] = len(blocks)
            top = block.astype(ml_dtypes.bfloat16)
            rest = (block - top.astype(np.float32)).astype(ml_dtypes.bfloat16)
            blocks.append((top, rest))
        places.append((start, stop, first, last, seen[key]))
    return blocks, places


def kernel(sizes, places, nblocks, *refs):
    tm_count, ang_count, ax_count = sizes
    steps_ref, reluct_ref, resist_ref, rates_ref, s_hbm, q_hbm, ids_hbm = refs[:7]
    w_hbm = refs[7 : 7 + 2 * nblocks]
    coarse_ref, rdif = refs[7 + 2 * nblocks : 9 + 2 * nblocks]
    (
        q_ref, ids_ref, u, ca, cc, cb, rc, xh, xl, ha, hz, sa, sz,
        gs, off, dif, other, fs, fp, inv, fe, fo,
        pair, pin, sin, pout, sout, mine, give,
        a_send, a_recv, z_send, z_recv, o_send, o_recv,
        d_send, d_recv, p_send, p_recv, q_send, q_recv, c_send, c_recv, in_sem, out_sem, *w_refs
    ) = refs[9 + 2 * nblocks :]
    na, nz, rad = u.shape
    half = na // 2
    part = half // 2
    regions = rates_ref.shape[0]
    tm, ang, ax = lax.axis_index("tm"), lax.axis_index("ang"), lax.axis_index("ax")
    core, chip = lax.rem(tm, 2), tm // 2
    chips = tm_count // 2
    mate = tm + 1 - 2 * core

    def ring(value, step, count):
        return lax.rem(value + step + count, count)

    loads = [(s_hbm.at[0], u), (ids_hbm, ids_ref), (q_hbm.at[0], q_ref), *zip(w_hbm, w_refs)]
    loads = [pltpu.make_async_copy(a, b, in_sem.at[n]) for n, (a, b) in enumerate(loads)]
    for load in loads:
        load.start()

    barrier = pltpu.get_barrier_semaphore()
    greet = [("ang", ang, 1, ang_count), ("ang", ang, -1, ang_count)]
    greet += [("ax", ax, 1, ax_count)]
    greet += [("tm", tm, step, tm_count) for step in (1, -1, 2, -2)]
    for axis, value, step, count in greet:
        pl.semaphore_signal(
            barrier, inc=1, device_id={axis: ring(value, step, count)},
            device_id_type=pl.DeviceIdType.MESH,
        )

    def remote(src, dst, send, recv, device):
        return pltpu.make_async_remote_copy(
            src_ref=src, dst_ref=dst, send_sem=send, recv_sem=recv,
            device_id=device, device_id_type=pl.DeviceIdType.MESH,
        )

    groups = [(places[a][0], places[b - 1][1]) for a, b in zip((0,) + GROUPS, GROUPS + (len(places),))]

    def ang_copy(t, block, side):
        lanes = slice(*groups[block])
        return remote(
            sa.at[t, side, :, lanes], ha.at[t, 1 - side, :, lanes],
            a_send.at[t, block, side], a_recv.at[t, block, 1 - side],
            {"ang": ring(ang, 2 * side - 1, ang_count)},
        )

    def ax_copy(t, block):
        lanes = slice(*groups[block])
        return remote(
            sz.at[t, :, lanes], hz.at[t, ax, :, lanes],
            z_send.at[t, block], z_recv.at[t, block], {"ax": 1 - ax},
        )

    def pack(t, block):
        lanes = slice(*groups[block])
        sa[t, 0, :, lanes] = u[0, :, lanes]
        sa[t, 1, :, lanes] = u[na - 1, :, lanes]

        for a in range(na):
            sz[t, a : a + 1, lanes] = jnp.where(ax == 0, u[a, nz - 1 : nz, lanes], u[a, 0:1, lanes])

    def send_halo(t, block):
        ang_copy(t, block, 0).start()
        ang_copy(t, block, 1).start()
        ax_copy(t, block).start()

    def wait_halo(t, block):
        ang_copy(t, block, 0).wait()
        ang_copy(t, block, 1).wait()
        ax_copy(t, block).wait()

    hz[:, ax] = jnp.zeros((STEPS, na, rad), F32)

    @pl.when(chip == 0)
    def _():
        pin[...] = jnp.zeros_like(pin)

    @pl.when(chip == chips - 1)
    def _():
        sin[...] = jnp.zeros_like(sin)

    loads[0].wait()
    for block in range(len(groups)):
        pack(0, block)
    pl.semaphore_wait(barrier, len(greet))
    for block in range(len(groups)):
        send_halo(0, block)

    loads[1].wait()
    loads[2].wait()
    reluct = [explicit_limit * reluct_ref[k] * resist_ref[k] for k in range(regions)]
    rates = [rates_ref[k] for k in range(regions)]
    own_steps = steps_ref[tm]

    def tables(a, _):
        for l in range(0, rad, LANES):
            cut = slice(l, l + LANES)
            ids = ids_ref[a, :, cut]
            coupling = jnp.zeros(ids.shape, F32)
            relax = jnp.zeros(ids.shape, F32)
            for k in range(regions):
                hit = ids == k
                coupling = jnp.where(hit, reluct[k], coupling)
                relax = jnp.where(hit, rates[k], relax)
            cc[a, :, cut] = coupling
            ca[a, :, cut] = 1.0 - 4.0 * coupling - relax
            cb[a, :, cut] = relax * q_ref[a, :, cut]
            previous = rc[a // 2, :, cut]
            rc[a // 2, :, cut] = jnp.where(lax.rem(a, 2) == 0, relax, 0.5 * (previous + relax))
        return 0

    lax.fori_loop(0, na, tables, 0)

    def own_factor(i, _):
        mean = (u[2 * i] + u[2 * i + 1]) * 0.5
        gs[i] = mean / (1.0 + own_steps.astype(F32) * rc[i])
        return 0

    lax.fori_loop(0, half, own_factor, 0)

    def factors(k, _):
        rate = rc[part * core + k]
        before = jnp.ones_like(rate)
        after = jnp.ones_like(rate)
        for j in range(tm_count):
            count = steps_ref[j].astype(F32)
            before = before * (1.0 + jnp.where(j < 2 * chip, count, 0.0) * rate)
            after = after * (1.0 + jnp.where(j > 2 * chip + 1, count, 0.0) * rate)
        even = 1.0 + steps_ref[2 * chip].astype(F32) * rate
        odd = 1.0 + steps_ref[2 * chip + 1].astype(F32) * rate
        whole = before * after * (even * odd)
        fs[k] = 1.0 / after
        fp[k] = 1.0 / before
        fe[k] = 1.0 / even
        fo[k] = 1.0 / odd
        inv[k] = whole / (whole - 1.0)
        return 0

    lax.fori_loop(0, part, factors, 0)
    for load in loads[3:]:
        load.wait()

    chunks = rad // CHUNK

    def lanes_of(k):
        return pl.ds(pl.multiple_of(k * CHUNK, CHUNK), CHUNK)

    ours, yours = pl.ds(part * core, part), pl.ds(part * (1 - core), part)

    def mate_copy(k):
        cut = lanes_of(k)
        return remote(
            off.at[yours, :, cut], other.at[:, :, cut], o_send.at[k], o_recv.at[k], {"tm": mate}
        )

    def change_copy(k):
        cut = lanes_of(k)
        return remote(
            dif.at[:, :, cut], rdif.at[:, :, cut], d_send.at[k], d_recv.at[k],
            {"tm": ring(tm, 1, tm_count)},
        )

    def forward_copy(k):
        cut = lanes_of(k)
        return remote(
            pout.at[:, :, cut], pin.at[:, :, cut], p_send.at[k], p_recv.at[k],
            {"tm": ring(tm, 2, tm_count)},
        )

    def backward_copy(k):
        cut = lanes_of(k)
        return remote(
            sout.at[:, :, cut], sin.at[:, :, cut], q_send.at[k], q_recv.at[k],
            {"tm": ring(tm, -2, tm_count)},
        )

    def coarse_copy(k):
        cut = lanes_of(k)
        return remote(
            give.at[:, :, cut], coarse_ref.at[ours, :, cut], c_send.at[k], c_recv.at[k], {"tm": mate}
        )

    def keep_copy(k):
        cut = lanes_of(k)
        return pltpu.make_async_copy(mine.at[:, :, cut], coarse_ref.at[ours, :, cut], out_sem.at[k])

    def loop(body, first=0, last=chunks):
        def step(k, _):
            body(k)
            return 0

        lax.fori_loop(first, last, step, 0)

    def offsets(k):
        cut = lanes_of(k)
        for i in range(half):
            even, odd = u[2 * i, :, cut], u[2 * i + 1, :, cut]
            off[i, :, cut] = (even + odd) * 0.5 - gs[i, :, cut]
            dif[i, :, cut] = (even - odd) * 0.5
        mate_copy(k).start()

        @pl.when(core == 0)
        def _():
            change_copy(k).start()

    def fine(t, _):
        spot = lax.broadcasted_iota(jnp.int32, (TALL, CHUNK), 0)
        low_edge, high_edge = spot == 0, spot == TALL - 1

        def stencil(lanes):
            for l in range(*lanes, CHUNK):
                cut = slice(l, l + CHUNK)
                above, here = ha[t, 0, :, cut], u[0, :, cut]
                for a in range(na):
                    below = u[a + 1, :, cut] if a < na - 1 else ha[t, 1, :, cut]
                    pieces = [here[r : r + TALL] for r in range(0, nz, TALL)]
                    down = [pltpu.roll(piece, 1, 0) for piece in pieces]
                    up = [pltpu.roll(piece, TALL - 1, 0) for piece in pieces]
                    down = [hz[t, 0, a : a + 1, cut]] + down
                    up = up + [hz[t, 1, a : a + 1, cut]]
                    beside = [
                        jnp.where(low_edge, down[r], down[r + 1]) + jnp.where(high_edge, up[r + 1], up[r])
                        for r in range(len(pieces))
                    ]
                    beside = jnp.concatenate(beside, 0) + (above + below)
                    value = ca[a, :, cut] * here + cc[a, :, cut] * beside + cb[a, :, cut]
                    top = value.astype(BF16)
                    rows = slice(a * nz, (a + 1) * nz)
                    xh[rows, cut] = top
                    xl[rows, cut] = (value - top.astype(F32)).astype(BF16)
                    above, here = here, below

        ready, arrived = 0, 0
        for block, (start, stop, first, last, which) in enumerate(places):
            while arrived < len(groups) and groups[arrived][0] < last:
                wait_halo(t, arrived)
                arrived += 1
            if ready < last:
                stencil((ready, last))
                ready = last
            high, low = w_refs[2 * which], w_refs[2 * which + 1]
            left, rest = xh[:, first:last], xl[:, first:last]
            fields = jnp.concatenate([left, rest, left], 1)
            weights = jnp.concatenate([high[...], high[...], low[...]], 0)
            total = jnp.dot(fields, weights, preferred_element_type=F32)
            total = total.reshape(na, nz, stop - start)
            active = jnp.full(total.shape, own_steps, jnp.int32) > t
            u[:, :, start:stop] = jnp.where(active, total, u[:, :, start:stop])

            for group, (_, end) in enumerate(groups):
                if end == stop:

                    @pl.when(t < STEPS - 1)
                    def _():
                        pack(t + 1, group)
                        send_halo(t + 1, group)

            @pl.when(t == STEPS - 1)
            def _():
                loop(offsets, start // CHUNK, stop // CHUNK)

        return 0

    lax.fori_loop(0, STEPS, fine, 0)

    ends = (chip == 0) | (chip == chips - 1)
    near_odd = jnp.logical_not(ends) & (core == 1)

    def pairs(k):
        mate_copy(k).wait()
        cut = lanes_of(k)
        own, theirs = off[ours, :, cut], other[:, :, cut]
        even = jnp.where(core == 0, own, theirs)
        odd = jnp.where(core == 0, theirs, own)
        pair[:, :, cut] = fo[:, :, cut] * even + odd

    def forward(k):
        cut = lanes_of(k)

        @pl.when(chip > 0)
        def _():
            forward_copy(k).wait_recv()

        pout[:, :, cut] = fe[:, :, cut] * fo[:, :, cut] * pin[:, :, cut] + pair[:, :, cut]

        @pl.when(chip < chips - 1)
        def _():
            forward_copy(k).start()

    def backward(k):
        cut = lanes_of(k)

        @pl.when(chip < chips - 1)
        def _():
            backward_copy(k).wait_recv()

        sout[:, :, cut] = fs[:, :, cut] * pair[:, :, cut] + sin[:, :, cut]

        @pl.when(chip > 0)
        def _():
            backward_copy(k).start()

    def settle(k):
        cut = lanes_of(k)
        own, theirs = off[ours, :, cut], other[:, :, cut]
        first = jnp.where(core == 0, own, theirs)
        even = (fp[:, :, cut] * sout[:, :, cut] + pin[:, :, cut]) * inv[:, :, cut]
        odd = fe[:, :, cut] * even + first
        mine[:, :, cut] = jnp.where(core == 0, even, odd)
        give[:, :, cut] = jnp.where(core == 0, odd, even)
        coarse_copy(k).start()
        keep_copy(k).start()

    def send_change(k):
        change_copy(k).start()

    @pl.when(near_odd)
    def _():
        loop(send_change, 0, AHEAD)

    def both(first, second):
        def one(k):
            pairs(k)

            @pl.when(near_odd & (k + AHEAD < chunks))
            def _():
                send_change(k + AHEAD)

            first(k)

        def two(k):
            second(k)
            settle(k)

        @pl.when(ends)
        def _():
            loop(one)

            @pl.when(core == 1)
            def _():
                loop(send_change)

            loop(two)

        @pl.when(jnp.logical_not(ends))
        def _():
            loop(one, 0, LAG)

            def step(k):
                one(k)
                two(k - LAG)

            loop(step, LAG, chunks)
            loop(two, chunks - LAG, chunks)

    @pl.when(chip < chips // 2)
    def _():
        both(forward, backward)

    @pl.when(chip >= chips // 2)
    def _():
        both(backward, forward)

    def finish(k):
        keep_copy(k).wait()
        coarse_copy(k).wait()
        change_copy(k).wait()

        @pl.when(chip < chips - 1)
        def _():
            forward_copy(k).wait_send()

        @pl.when(chip > 0)
        def _():
            backward_copy(k).wait_send()

    loop(finish)


def spread(coarse_ref, change_ref, out_ref):
    for r in range(coarse_ref.shape[0]):
        out_ref[0, 2 * r] = coarse_ref[r] + change_ref[r]
        out_ref[0, 2 * r + 1] = coarse_ref[r] - change_ref[r]


def solution(mesh):
    sizes = tuple(mesh.shape[name] for name in ("tm", "ang", "ax"))

    def local(starts, drive, region_ids, steps, reluctivity, resistivity, rates):
        na, nz, rad = region_ids.shape
        half, part = na // 2, na // 4
        blocks, places = inverse_blocks(rad)
        weights = [jnp.asarray(piece) for block in blocks for piece in block]
        smem = pl.BlockSpec(memory_space=pltpu.SMEM)
        anywhere = pl.BlockSpec(memory_space=pltpu.HBM)

        def field(*lead):
            return pltpu.VMEM(lead + (nz, rad), F32)

        halo = pltpu.VMEM((STEPS, 2, nz, rad), F32)
        axial = pltpu.VMEM((STEPS, 2, na, rad), F32)
        face = pltpu.VMEM((STEPS, na, rad), F32)
        dma = pltpu.SemaphoreType.DMA
        scratch = [
            field(na), pltpu.VMEM((na, nz, rad), jnp.int32),
            field(na), field(na), field(na), field(na), field(half),
            pltpu.VMEM((na * nz, rad), BF16), pltpu.VMEM((na * nz, rad), BF16),
            halo, axial, halo, face,
            field(half), field(half), field(half), field(part),
        ]
        scratch += [field(part)] * 5 + [field(part)] * 7
        scratch += [dma((STEPS, len(GROUPS) + 1, 2))] * 2 + [dma((STEPS, len(GROUPS) + 1))] * 2 + [dma((rad // CHUNK,))] * 10
        scratch += [dma((3 + len(weights),)), dma((rad // CHUNK,))]
        scratch += [pltpu.VMEM(piece.shape, BF16) for piece in weights]
        pairs = jax.ShapeDtypeStruct((half, nz, rad), F32)
        coarse, change = pl.pallas_call(
            functools.partial(kernel, sizes, places, len(blocks)),
            out_shape=(pairs, pairs),
            in_specs=[smem] * 4 + [anywhere] * (3 + len(weights)),
            out_specs=[pl.BlockSpec(memory_space=pl.ANY)] * 2,
            scratch_shapes=scratch,
            compiler_params=pltpu.CompilerParams(
                collective_id=0, has_side_effects=True, vmem_limit_bytes=VMEM_LIMIT
            ),
        )(steps, reluctivity, resistivity, rates, starts, drive, region_ids, *weights)
        rows = half // SPLIT
        narrow = pl.BlockSpec((rows, nz, rad), lambda i: (i, 0, 0))
        return pl.pallas_call(
            spread,
            grid=(SPLIT,),
            out_shape=jax.ShapeDtypeStruct(starts.shape, F32),
            in_specs=[narrow] * 2,
            out_specs=pl.BlockSpec((1, 2 * rows, nz, rad), lambda i: (0, i, 0, 0)),
        )(coarse, change)

    cells = P("tm", "ang", "ax", None)
    placed = (cells, cells, P("ang", "ax", None), P(), P(), P(), P())
    return jax.shard_map(local, mesh=mesh, in_specs=placed, out_specs=cells, check_vma=False)
```

```python
import functools

import jax
import jax.numpy as jnp
import ml_dtypes
import numpy as np
from jax import lax
from jax.experimental import pallas as pl
from jax.experimental.pallas import tpu as pltpu
from jax.sharding import PartitionSpec as P

STEPS = 4
LANES = 384
WIDE = 256
EDGE = 128
CHUNK = 128
TALL = 8
SPLIT = 2
VMEM_LIMIT = 60 * 2**20
AHEAD = 5
LAG = 5
GROUPS = (1, 2, 3, 4)

radial_weight = 1.0
explicit_limit = 0.23
F32 = jnp.float32
BF16 = jnp.bfloat16


def inverse_blocks(size):
    middle = 2.0 + 1.0 / radial_weight
    r = (middle - np.sqrt(middle * middle - 4.0)) / 2.0
    index = np.arange(size, dtype=np.float64)
    low = np.minimum(index[:, None], index[None, :])
    high = np.maximum(index[:, None], index[None, :])
    full = r ** (high - low) * (1 - r ** (2 * low + 2)) * (1 - r ** (2 * (size - high)))
    full = full / ((1 / r - r) * (1 - r ** (2 * size + 2)) * radial_weight)
    full = full.astype(np.float32)
    blocks, places, seen = [], [], {}
    for start in range(0, size, WIDE):
        stop = min(start + WIDE, size)
        first, last = max(start - EDGE, 0), min(stop + EDGE, size)
        block = np.ascontiguousarray(full[first:last, start:stop])
        key = (block.shape, block.tobytes())
        if key not in seen:
            seen[key] = len(blocks)
            top = block.astype(ml_dtypes.bfloat16)
            rest = (block - top.astype(np.float32)).astype(ml_dtypes.bfloat16)
            blocks.append((top, rest))
        places.append((start, stop, first, last, seen[key]))
    return blocks, places


def kernel(sizes, places, nblocks, *refs):
    tm_count, ang_count, ax_count = sizes
    steps_ref, reluct_ref, resist_ref, rates_ref, s_hbm, q_hbm, ids_hbm = refs[:7]
    w_hbm = refs[7 : 7 + 2 * nblocks]
    coarse_ref, rdif = refs[7 + 2 * nblocks : 9 + 2 * nblocks]
    (
        q_ref, ids_ref, u, ca, cc, cb, rc, xh, xl, bh, bl, ha, hz, sz, inner, fa, fc, fb,
        gs, off, dif, other, fs, fp, inv, fe, fo,
        pair, pin, sin, pout, sout, mine, give,
        a_send, a_recv, z_send, z_recv, o_send, o_recv,
        d_send, d_recv, p_send, p_recv, q_send, q_recv, c_send, c_recv, in_sem, out_sem, *w_refs
    ) = refs[9 + 2 * nblocks :]
    na, nz, rad = ids_ref.shape
    half = na // 2
    part = half // 2
    regions = rates_ref.shape[0]
    tm, ang, ax = lax.axis_index("tm"), lax.axis_index("ang"), lax.axis_index("ax")
    core, chip = lax.rem(tm, 2), tm // 2
    chips = tm_count // 2
    mate = tm + 1 - 2 * core

    def ring(value, step, count):
        return lax.rem(value + step + count, count)

    loads = [(s_hbm.at[0], u.at[0]), (ids_hbm, ids_ref), (q_hbm.at[0], q_ref), *zip(w_hbm, w_refs)]
    loads = [pltpu.make_async_copy(a, b, in_sem.at[n]) for n, (a, b) in enumerate(loads)]
    for load in loads:
        load.start()

    barrier = pltpu.get_barrier_semaphore()
    greet = [("ang", ang, 1, ang_count), ("ang", ang, -1, ang_count)]
    greet += [("ax", ax, 1, ax_count)]
    greet += [("tm", tm, step, tm_count) for step in (1, -1, 2, -2)]
    for axis, value, step, count in greet:
        pl.semaphore_signal(
            barrier, inc=1, device_id={axis: ring(value, step, count)},
            device_id_type=pl.DeviceIdType.MESH,
        )

    def remote(src, dst, send, recv, device):
        return pltpu.make_async_remote_copy(
            src_ref=src, dst_ref=dst, send_sem=send, recv_sem=recv,
            device_id=device, device_id_type=pl.DeviceIdType.MESH,
        )

    groups = [(places[a][0], places[b - 1][1]) for a, b in zip((0,) + GROUPS, GROUPS + (len(places),))]

    def ang_copy(t, block, side):
        lanes = slice(*groups[block])
        return remote(
            u.at[lax.rem(t, 2), (na - 1) * side, :, lanes], ha.at[t, 1 - side, :, lanes],
            a_send.at[t, block, side], a_recv.at[t, block, 1 - side],
            {"ang": ring(ang, 2 * side - 1, ang_count)},
        )

    def ax_copy(t, block):
        lanes = slice(*groups[block])
        return remote(
            sz.at[t, :, lanes], hz.at[t, :, lanes],
            z_send.at[t, block], z_recv.at[t, block], {"ax": 1 - ax},
        )

    def send_halo(t, block):
        ang_copy(t, block, 0).start()
        ang_copy(t, block, 1).start()
        ax_copy(t, block).start()

    def wait_halo(t, block):
        ang_copy(t, block, 0).wait()
        ang_copy(t, block, 1).wait()
        ax_copy(t, block).wait()

    def by_side(body):
        @pl.when(ax == 0)
        def _():
            body(nz - 1, nz - 2)

        @pl.when(ax == 1)
        def _():
            body(0, 1)

    def gather(field, face, into):
        for a in range(na):
            into[a : a + 1, :] = field[a, face : face + 1, :]

    @pl.when(chip == 0)
    def _():
        pin[...] = jnp.zeros_like(pin)

    @pl.when(chip == chips - 1)
    def _():
        sin[...] = jnp.zeros_like(sin)

    loads[0].wait()
    by_side(lambda face, near: gather(u.at[0], face, sz.at[0]))
    pl.semaphore_wait(barrier, len(greet))
    for block in range(len(groups)):
        send_halo(0, block)

    loads[1].wait()
    loads[2].wait()
    reluct = [explicit_limit * reluct_ref[k] * resist_ref[k] for k in range(regions)]
    rates = [rates_ref[k] for k in range(regions)]
    own_steps = steps_ref[tm]

    def tables(a, _):
        for l in range(0, rad, LANES):
            cut = slice(l, l + LANES)
            ids = ids_ref[a, :, cut]
            coupling = jnp.zeros(ids.shape, F32)
            relax = jnp.zeros(ids.shape, F32)
            for k in range(regions):
                hit = ids == k
                coupling = jnp.where(hit, reluct[k], coupling)
                relax = jnp.where(hit, rates[k], relax)
            cc[a, :, cut] = coupling
            ca[a, :, cut] = 1.0 - 4.0 * coupling - relax
            cb[a, :, cut] = relax * q_ref[a, :, cut]
            previous = rc[a // 2, :, cut]
            rc[a // 2, :, cut] = jnp.where(lax.rem(a, 2) == 0, relax, 0.5 * (previous + relax))
        return 0

    lax.fori_loop(0, na, tables, 0)

    def side_tables(face, near):
        for field, into in ((ca, fa), (cc, fc), (cb, fb)):
            gather(field, face, into)

    by_side(side_tables)

    def own_factor(i, _):
        mean = (u[0, 2 * i] + u[0, 2 * i + 1]) * 0.5
        gs[i] = mean / (1.0 + own_steps.astype(F32) * rc[i])
        return 0

    lax.fori_loop(0, half, own_factor, 0)

    def factors(k, _):
        rate = rc[part * core + k]
        before = jnp.ones_like(rate)
        after = jnp.ones_like(rate)
        for j in range(tm_count):
            count = steps_ref[j].astype(F32)
            before = before * (1.0 + jnp.where(j < 2 * chip, count, 0.0) * rate)
            after = after * (1.0 + jnp.where(j > 2 * chip + 1, count, 0.0) * rate)
        even = 1.0 + steps_ref[2 * chip].astype(F32) * rate
        odd = 1.0 + steps_ref[2 * chip + 1].astype(F32) * rate
        whole = before * after * (even * odd)
        fs[k] = 1.0 / after
        fp[k] = 1.0 / before
        fe[k] = 1.0 / even
        fo[k] = 1.0 / odd
        inv[k] = whole / (whole - 1.0)
        return 0

    lax.fori_loop(0, part, factors, 0)
    for load in loads[3:]:
        load.wait()

    chunks = rad // CHUNK

    def lanes_of(k):
        return pl.ds(pl.multiple_of(k * CHUNK, CHUNK), CHUNK)

    ours, yours = pl.ds(part * core, part), pl.ds(part * (1 - core), part)

    def mate_copy(k):
        cut = lanes_of(k)
        return remote(
            off.at[yours, :, cut], other.at[:, :, cut], o_send.at[k], o_recv.at[k], {"tm": mate}
        )

    def change_copy(k):
        cut = lanes_of(k)
        return remote(
            dif.at[:, :, cut], rdif.at[:, :, cut], d_send.at[k], d_recv.at[k],
            {"tm": ring(tm, 1, tm_count)},
        )

    def forward_copy(k):
        cut = lanes_of(k)
        return remote(
            pout.at[:, :, cut], pin.at[:, :, cut], p_send.at[k], p_recv.at[k],
            {"tm": ring(tm, 2, tm_count)},
        )

    def backward_copy(k):
        cut = lanes_of(k)
        return remote(
            sout.at[:, :, cut], sin.at[:, :, cut], q_send.at[k], q_recv.at[k],
            {"tm": ring(tm, -2, tm_count)},
        )

    def coarse_copy(k):
        cut = lanes_of(k)
        return remote(
            give.at[:, :, cut], coarse_ref.at[ours, :, cut], c_send.at[k], c_recv.at[k], {"tm": mate}
        )

    def keep_copy(k):
        cut = lanes_of(k)
        return pltpu.make_async_copy(mine.at[:, :, cut], coarse_ref.at[ours, :, cut], out_sem.at[k])

    def loop(body, first=0, last=chunks):
        def step(k, _):
            body(k)
            return 0

        lax.fori_loop(first, last, step, 0)

    def offsets(k):
        cut = lanes_of(k)
        for i in range(half):
            even, odd = u[STEPS % 2, 2 * i, :, cut], u[STEPS % 2, 2 * i + 1, :, cut]
            off[i, :, cut] = (even + odd) * 0.5 - gs[i, :, cut]
            dif[i, :, cut] = (even - odd) * 0.5
        mate_copy(k).start()

        @pl.when(core == 0)
        def _():
            change_copy(k).start()

    spot = lax.broadcasted_iota(jnp.int32, (TALL, CHUNK), 0)
    low_edge, high_edge = spot == 0, spot == TALL - 1

    def shifted(here, before, after):
        pieces = [here[r : r + TALL] for r in range(0, here.shape[0], TALL)]
        down = [before] + [pltpu.roll(piece, 1, 0) for piece in pieces]
        up = [pltpu.roll(piece, TALL - 1, 0) for piece in pieces] + [after]
        both = [
            jnp.where(low_edge, down[r], down[r + 1]) + jnp.where(high_edge, up[r + 1], up[r])
            for r in range(len(pieces))
        ]
        return jnp.concatenate(both, 0)

    def split(value, rows, cut, high, low):
        top = value.astype(BF16)
        high[rows, cut] = top
        low[rows, cut] = (value - top.astype(F32)).astype(BF16)

    def solve(place, high, low):
        _, _, first, last, which = place
        top, rest = w_refs[2 * which][...], w_refs[2 * which + 1][...]
        left = high[:, first:last]
        fields = jnp.concatenate([left, low[:, first:last], left], 1)
        return jnp.dot(fields, jnp.concatenate([top, top, rest], 0), preferred_element_type=F32)

    def inside(t, now, later):
        def stencil(cut):
            above, here = u[now, 0, :, cut], u[now, 1, :, cut]
            for a in range(1, na - 1):
                below = u[now, a + 1, :, cut]
                beside = shifted(here, 0.0, 0.0) + (above + below)
                value = ca[a, :, cut] * here + cc[a, :, cut] * beside + cb[a, :, cut]
                split(value, slice((a - 1) * nz, a * nz), cut, xh, xl)
                above, here = here, below

        ready = 0
        for place in places:
            start, stop, _, last, _ = place
            for l in range(ready, last, CHUNK):
                stencil(slice(l, l + CHUNK))
            ready = max(ready, last)
            total = solve(place, xh, xl).reshape(na - 2, nz, stop - start)
            active = jnp.full(total.shape, own_steps, jnp.int32) > t
            u[later, 1 : na - 1, :, start:stop] = jnp.where(active, total, u[now, 1 : na - 1, :, start:stop])

    def border(t, now, later):
        def stencil(cut):
            for n, a, above, below in (
                (0, 0, ha[t, 0, :, cut], u[now, 1, :, cut]),
                (1, na - 1, u[now, na - 2, :, cut], ha[t, 1, :, cut]),
            ):
                here = u[now, a, :, cut]
                outer = hz[t, a : a + 1, cut]
                before, after = jnp.where(ax == 0, 0.0, outer), jnp.where(ax == 0, outer, 0.0)
                beside = shifted(here, before, after) + (above + below)
                value = ca[a, :, cut] * here + cc[a, :, cut] * beside + cb[a, :, cut]
                split(value, slice(n * nz, (n + 1) * nz), cut, bh, bl)
            before, after = (
                jnp.where(ax == 0, ha[t, side, nz - 1 : nz, cut], ha[t, side, 0:1, cut]) for side in (0, 1)
            )
            here = sz[t, :, cut]
            beside = shifted(here, before, after) + (inner[:, cut] + hz[t, :, cut])
            value = fa[:, cut] * here + fc[:, cut] * beside + fb[:, cut]
            split(value, slice(2 * nz, 2 * nz + na), cut, bh, bl)

        ready, arrived = 0, 0
        for place in places:
            start, stop, _, last, _ = place
            cut = slice(start, stop)
            while arrived < len(groups) and groups[arrived][0] < last:
                wait_halo(t, arrived)
                arrived += 1
            for l in range(ready, last, CHUNK):
                stencil(slice(l, l + CHUNK))
            ready = max(ready, last)
            total = solve(place, bh, bl)
            old = jnp.concatenate([u[now, 0, :, cut], u[now, na - 1, :, cut], sz[t, :, cut]], 0)
            total = jnp.where(jnp.full(total.shape, own_steps, jnp.int32) > t, total, old)
            u[later, 0, :, cut] = total[:nz]
            u[later, na - 1, :, cut] = total[nz : 2 * nz]
            sz[t + 1, :, cut] = total[2 * nz :]

            for group, (_, end) in enumerate(groups):
                if end == stop:

                    @pl.when(t < STEPS - 1)
                    def _():
                        send_halo(t + 1, group)

            def scatter(face, near):
                for a in range(1, na - 1):
                    u[later, a, face : face + 1, cut] = sz[t + 1, a : a + 1, cut]

            by_side(scatter)

            @pl.when(t == STEPS - 1)
            def _():
                loop(offsets, start // CHUNK, stop // CHUNK)

    def fine(t, _):
        now, later = lax.rem(t, 2), lax.rem(t + 1, 2)
        inside(t, now, later)
        by_side(lambda face, near: gather(u.at[now], near, inner))
        border(t, now, later)
        return 0

    lax.fori_loop(0, STEPS, fine, 0)

    ends = (chip == 0) | (chip == chips - 1)
    near_odd = jnp.logical_not(ends) & (core == 1)

    def pairs(k):
        mate_copy(k).wait()
        cut = lanes_of(k)
        own, theirs = off[ours, :, cut], other[:, :, cut]
        even = jnp.where(core == 0, own, theirs)
        odd = jnp.where(core == 0, theirs, own)
        pair[:, :, cut] = fo[:, :, cut] * even + odd

    def forward(k):
        cut = lanes_of(k)

        @pl.when(chip > 0)
        def _():
            forward_copy(k).wait_recv()

        pout[:, :, cut] = fe[:, :, cut] * fo[:, :, cut] * pin[:, :, cut] + pair[:, :, cut]

        @pl.when(chip < chips - 1)
        def _():
            forward_copy(k).start()

    def backward(k):
        cut = lanes_of(k)

        @pl.when(chip < chips - 1)
        def _():
            backward_copy(k).wait_recv()

        sout[:, :, cut] = fs[:, :, cut] * pair[:, :, cut] + sin[:, :, cut]

        @pl.when(chip > 0)
        def _():
            backward_copy(k).start()

    def settle(k):
        cut = lanes_of(k)
        own, theirs = off[ours, :, cut], other[:, :, cut]
        first = jnp.where(core == 0, own, theirs)
        even = (fp[:, :, cut] * sout[:, :, cut] + pin[:, :, cut]) * inv[:, :, cut]
        odd = fe[:, :, cut] * even + first
        mine[:, :, cut] = jnp.where(core == 0, even, odd)
        give[:, :, cut] = jnp.where(core == 0, odd, even)
        coarse_copy(k).start()
        keep_copy(k).start()

    def send_change(k):
        change_copy(k).start()

    @pl.when(near_odd)
    def _():
        loop(send_change, 0, AHEAD)

    def both(first, second):
        def one(k):
            pairs(k)

            @pl.when(near_odd & (k + AHEAD < chunks))
            def _():
                send_change(k + AHEAD)

            first(k)

        def two(k):
            second(k)
            settle(k)

        @pl.when(ends)
        def _():
            loop(one)

            @pl.when(core == 1)
            def _():
                loop(send_change)

            loop(two)

        @pl.when(jnp.logical_not(ends))
        def _():
            loop(one, 0, LAG)

            def step(k):
                one(k)
                two(k - LAG)

            loop(step, LAG, chunks)
            loop(two, chunks - LAG, chunks)

    @pl.when(chip < chips // 2)
    def _():
        both(forward, backward)

    @pl.when(chip >= chips // 2)
    def _():
        both(backward, forward)

    def finish(k):
        keep_copy(k).wait()
        coarse_copy(k).wait()
        change_copy(k).wait()

        @pl.when(chip < chips - 1)
        def _():
            forward_copy(k).wait_send()

        @pl.when(chip > 0)
        def _():
            backward_copy(k).wait_send()

    loop(finish)


def spread(coarse_ref, change_ref, out_ref):
    for r in range(coarse_ref.shape[0]):
        out_ref[0, 2 * r] = coarse_ref[r] + change_ref[r]
        out_ref[0, 2 * r + 1] = coarse_ref[r] - change_ref[r]


def solution(mesh):
    sizes = tuple(mesh.shape[name] for name in ("tm", "ang", "ax"))

    def local(starts, drive, region_ids, steps, reluctivity, resistivity, rates):
        na, nz, rad = region_ids.shape
        half, part = na // 2, na // 4
        blocks, places = inverse_blocks(rad)
        weights = [jnp.asarray(piece) for block in blocks for piece in block]
        smem = pl.BlockSpec(memory_space=pltpu.SMEM)
        anywhere = pl.BlockSpec(memory_space=pltpu.HBM)

        def field(*lead):
            return pltpu.VMEM(lead + (nz, rad), F32)

        halo = pltpu.VMEM((STEPS, 2, nz, rad), F32)
        face = pltpu.VMEM((STEPS, na, rad), F32)
        dma = pltpu.SemaphoreType.DMA
        edge = pltpu.VMEM((na, rad), F32)
        inside = pltpu.VMEM(((na - 2) * nz, rad), BF16)
        border = pltpu.VMEM((2 * nz + na, rad), BF16)
        scratch = [
            field(na), pltpu.VMEM((na, nz, rad), jnp.int32),
            field(2, na), field(na), field(na), field(na), field(half),
            inside, inside, border, border,
            halo, face, pltpu.VMEM((STEPS + 1, na, rad), F32), edge, edge, edge, edge,
            field(half), field(half), field(half), field(part),
        ]
        scratch += [field(part)] * 5 + [field(part)] * 7
        scratch += [dma((STEPS, len(GROUPS) + 1, 2))] * 2 + [dma((STEPS, len(GROUPS) + 1))] * 2 + [dma((rad // CHUNK,))] * 10
        scratch += [dma((3 + len(weights),)), dma((rad // CHUNK,))]
        scratch += [pltpu.VMEM(piece.shape, BF16) for piece in weights]
        pairs = jax.ShapeDtypeStruct((half, nz, rad), F32)
        coarse, change = pl.pallas_call(
            functools.partial(kernel, sizes, places, len(blocks)),
            out_shape=(pairs, pairs),
            in_specs=[smem] * 4 + [anywhere] * (3 + len(weights)),
            out_specs=[pl.BlockSpec(memory_space=pl.ANY)] * 2,
            scratch_shapes=scratch,
            compiler_params=pltpu.CompilerParams(
                collective_id=0, has_side_effects=True, vmem_limit_bytes=VMEM_LIMIT
            ),
        )(steps, reluctivity, resistivity, rates, starts, drive, region_ids, *weights)
        rows = half // SPLIT
        narrow = pl.BlockSpec((rows, nz, rad), lambda i: (i, 0, 0))
        return pl.pallas_call(
            spread,
            grid=(SPLIT,),
            out_shape=jax.ShapeDtypeStruct(starts.shape, F32),
            in_specs=[narrow] * 2,
            out_specs=pl.BlockSpec((1, 2 * rows, nz, rad), lambda i: (0, i, 0, 0)),
        )(coarse, change)

    cells = P("tm", "ang", "ax", None)
    placed = (cells, cells, P("ang", "ax", None), P(), P(), P(), P())
    return jax.shard_map(local, mesh=mesh, in_specs=placed, out_specs=cells, check_vma=False)
```

```python
import functools

import jax
import jax.numpy as jnp
import ml_dtypes
import numpy as np
from jax import lax
from jax.experimental import pallas as pl
from jax.experimental.pallas import tpu as pltpu
from jax.sharding import PartitionSpec as P

STEPS = 4
LANES = 384
WIDE = 256
EDGE = 128
CHUNK = 128
TALL = 8
SPLIT = 2
VMEM_LIMIT = 60 * 2**20
AHEAD = 5
LAG = 5
BURST = 6
RATE = (1, 2)
GROUPS = (1, 2, 3, 4)

radial_weight = 1.0
explicit_limit = 0.23
F32 = jnp.float32
BF16 = jnp.bfloat16


def inverse_blocks(size):
    middle = 2.0 + 1.0 / radial_weight
    r = (middle - np.sqrt(middle * middle - 4.0)) / 2.0
    index = np.arange(size, dtype=np.float64)
    low = np.minimum(index[:, None], index[None, :])
    high = np.maximum(index[:, None], index[None, :])
    full = r ** (high - low) * (1 - r ** (2 * low + 2)) * (1 - r ** (2 * (size - high)))
    full = full / ((1 / r - r) * (1 - r ** (2 * size + 2)) * radial_weight)
    full = full.astype(np.float32)
    blocks, places, seen = [], [], {}
    for start in range(0, size, WIDE):
        stop = min(start + WIDE, size)
        first, last = max(start - EDGE, 0), min(stop + EDGE, size)
        block = np.ascontiguousarray(full[first:last, start:stop])
        key = (block.shape, block.tobytes())
        if key not in seen:
            seen[key] = len(blocks)
            top = block.astype(ml_dtypes.bfloat16)
            rest = (block - top.astype(np.float32)).astype(ml_dtypes.bfloat16)
            blocks.append((top, rest))
        places.append((start, stop, first, last, seen[key]))
    return blocks, places


def kernel(sizes, places, nblocks, *refs):
    tm_count, ang_count, ax_count = sizes
    steps_ref, reluct_ref, resist_ref, rates_ref, s_hbm, q_hbm, ids_hbm = refs[:7]
    w_hbm = refs[7 : 7 + 2 * nblocks]
    coarse_ref, rdif = refs[7 + 2 * nblocks : 9 + 2 * nblocks]
    (
        q_ref, ids_ref, u, ca, cc, cb, rc, xh, xl, bh, bl, ha, hz, sz, inner, fa, fc, fb,
        gs, off, dif, other, fs, fp, inv, fe, fo,
        pair, pin, sin, pout, sout, mine, give,
        a_send, a_recv, z_send, z_recv, o_send, o_recv,
        d_send, d_recv, p_send, p_recv, q_send, q_recv, c_send, c_recv, in_sem, out_sem, *w_refs
    ) = refs[9 + 2 * nblocks :]
    na, nz, rad = ids_ref.shape
    half = na // 2
    part = half // 2
    regions = rates_ref.shape[0]
    tm, ang, ax = lax.axis_index("tm"), lax.axis_index("ang"), lax.axis_index("ax")
    core, chip = lax.rem(tm, 2), tm // 2
    chips = tm_count // 2
    mate = tm + 1 - 2 * core

    def ring(value, step, count):
        return lax.rem(value + step + count, count)

    loads = [(s_hbm.at[0], u.at[0]), (ids_hbm, ids_ref), (q_hbm.at[0], q_ref), *zip(w_hbm, w_refs)]
    loads = [pltpu.make_async_copy(a, b, in_sem.at[n]) for n, (a, b) in enumerate(loads)]
    for load in loads:
        load.start()

    barrier = pltpu.get_barrier_semaphore()
    greet = [("ang", ang, 1, ang_count), ("ang", ang, -1, ang_count)]
    greet += [("ax", ax, 1, ax_count)]
    greet += [("tm", tm, step, tm_count) for step in (1, -1, 2, -2)]
    for axis, value, step, count in greet:
        pl.semaphore_signal(
            barrier, inc=1, device_id={axis: ring(value, step, count)},
            device_id_type=pl.DeviceIdType.MESH,
        )

    def remote(src, dst, send, recv, device):
        return pltpu.make_async_remote_copy(
            src_ref=src, dst_ref=dst, send_sem=send, recv_sem=recv,
            device_id=device, device_id_type=pl.DeviceIdType.MESH,
        )

    groups = [(places[a][0], places[b - 1][1]) for a, b in zip((0,) + GROUPS, GROUPS + (len(places),))]

    def ang_copy(t, block, side):
        lanes = slice(*groups[block])
        return remote(
            u.at[lax.rem(t, 2), (na - 1) * side, :, lanes], ha.at[t, 1 - side, :, lanes],
            a_send.at[t, block, side], a_recv.at[t, block, 1 - side],
            {"ang": ring(ang, 2 * side - 1, ang_count)},
        )

    def ax_copy(t, block):
        lanes = slice(*groups[block])
        return remote(
            sz.at[t, :, lanes], hz.at[t, :, lanes],
            z_send.at[t, block], z_recv.at[t, block], {"ax": 1 - ax},
        )

    def send_halo(t, block):
        ang_copy(t, block, 0).start()
        ang_copy(t, block, 1).start()
        ax_copy(t, block).start()

    def wait_halo(t, block):
        ang_copy(t, block, 0).wait()
        ang_copy(t, block, 1).wait()
        ax_copy(t, block).wait()

    def by_side(body):
        @pl.when(ax == 0)
        def _():
            body(nz - 1, nz - 2)

        @pl.when(ax == 1)
        def _():
            body(0, 1)

    def gather(field, face, into):
        for a in range(na):
            into[a : a + 1, :] = field[a, face : face + 1, :]

    @pl.when(chip == 0)
    def _():
        pin[...] = jnp.zeros_like(pin)

    @pl.when(chip == chips - 1)
    def _():
        sin[...] = jnp.zeros_like(sin)

    loads[0].wait()
    by_side(lambda face, near: gather(u.at[0], face, sz.at[0]))
    pl.semaphore_wait(barrier, len(greet))
    for block in range(len(groups)):
        send_halo(0, block)

    loads[1].wait()
    loads[2].wait()
    reluct = [explicit_limit * reluct_ref[k] * resist_ref[k] for k in range(regions)]
    rates = [rates_ref[k] for k in range(regions)]
    own_steps = steps_ref[tm]

    def tables(a, _):
        for l in range(0, rad, LANES):
            cut = slice(l, l + LANES)
            ids = ids_ref[a, :, cut]
            coupling = jnp.zeros(ids.shape, F32)
            relax = jnp.zeros(ids.shape, F32)
            for k in range(regions):
                hit = ids == k
                coupling = jnp.where(hit, reluct[k], coupling)
                relax = jnp.where(hit, rates[k], relax)
            cc[a, :, cut] = coupling
            ca[a, :, cut] = 1.0 - 4.0 * coupling - relax
            cb[a, :, cut] = relax * q_ref[a, :, cut]
            previous = rc[a // 2, :, cut]
            rc[a // 2, :, cut] = jnp.where(lax.rem(a, 2) == 0, relax, 0.5 * (previous + relax))
        return 0

    lax.fori_loop(0, na, tables, 0)

    def side_tables(face, near):
        for field, into in ((ca, fa), (cc, fc), (cb, fb)):
            gather(field, face, into)

    by_side(side_tables)

    def own_factor(i, _):
        mean = (u[0, 2 * i] + u[0, 2 * i + 1]) * 0.5
        gs[i] = mean / (1.0 + own_steps.astype(F32) * rc[i])
        return 0

    lax.fori_loop(0, half, own_factor, 0)

    def factors(k, _):
        rate = rc[part * core + k]
        before = jnp.ones_like(rate)
        after = jnp.ones_like(rate)
        for j in range(tm_count):
            count = steps_ref[j].astype(F32)
            before = before * (1.0 + jnp.where(j < 2 * chip, count, 0.0) * rate)
            after = after * (1.0 + jnp.where(j > 2 * chip + 1, count, 0.0) * rate)
        even = 1.0 + steps_ref[2 * chip].astype(F32) * rate
        odd = 1.0 + steps_ref[2 * chip + 1].astype(F32) * rate
        whole = before * after * (even * odd)
        fs[k] = 1.0 / after
        fp[k] = 1.0 / before
        fe[k] = 1.0 / even
        fo[k] = 1.0 / odd
        inv[k] = whole / (whole - 1.0)
        return 0

    lax.fori_loop(0, part, factors, 0)
    for load in loads[3:]:
        load.wait()

    chunks = rad // CHUNK

    def lanes_of(k):
        return pl.ds(pl.multiple_of(k * CHUNK, CHUNK), CHUNK)

    ours, yours = pl.ds(part * core, part), pl.ds(part * (1 - core), part)

    def mate_copy(k):
        cut = lanes_of(k)
        return remote(
            off.at[yours, :, cut], other.at[:, :, cut], o_send.at[k], o_recv.at[k], {"tm": mate}
        )

    def change_copy(k):
        cut = lanes_of(k)
        return remote(
            dif.at[:, :, cut], rdif.at[:, :, cut], d_send.at[k], d_recv.at[k],
            {"tm": ring(tm, 1, tm_count)},
        )

    def forward_copy(k):
        cut = lanes_of(k)
        return remote(
            pout.at[:, :, cut], pin.at[:, :, cut], p_send.at[k], p_recv.at[k],
            {"tm": ring(tm, 2, tm_count)},
        )

    def backward_copy(k):
        cut = lanes_of(k)
        return remote(
            sout.at[:, :, cut], sin.at[:, :, cut], q_send.at[k], q_recv.at[k],
            {"tm": ring(tm, -2, tm_count)},
        )

    def coarse_copy(k):
        cut = lanes_of(k)
        return remote(
            give.at[:, :, cut], coarse_ref.at[ours, :, cut], c_send.at[k], c_recv.at[k], {"tm": mate}
        )

    def keep_copy(k):
        cut = lanes_of(k)
        return pltpu.make_async_copy(mine.at[:, :, cut], coarse_ref.at[ours, :, cut], out_sem.at[k])

    def loop(body, first=0, last=chunks):
        def step(k, _):
            body(k)
            return 0

        lax.fori_loop(first, last, step, 0)

    ends = (chip == 0) | (chip == chips - 1)
    near_odd = jnp.logical_not(ends) & (core == 1)
    last_odd = (chip == chips - 1) & (core == 1)

    def due(k):
        return jnp.minimum(BURST + k * RATE[0] // RATE[1], chunks)

    def offsets(k):
        cut = lanes_of(k)
        for i in range(half):
            even, odd = u[STEPS % 2, 2 * i, :, cut], u[STEPS % 2, 2 * i + 1, :, cut]
            off[i, :, cut] = (even + odd) * 0.5 - gs[i, :, cut]
            dif[i, :, cut] = (even - odd) * 0.5
        mate_copy(k).start()

        soon = (core == 0) | (near_odd & (k < AHEAD)) | (last_odd & (k < BURST))

        @pl.when(soon)
        def _():
            change_copy(k).start()

    spot = lax.broadcasted_iota(jnp.int32, (TALL, CHUNK), 0)
    low_edge, high_edge = spot == 0, spot == TALL - 1

    def shifted(here, before, after):
        pieces = [here[r : r + TALL] for r in range(0, here.shape[0], TALL)]
        down = [before] + [pltpu.roll(piece, 1, 0) for piece in pieces]
        up = [pltpu.roll(piece, TALL - 1, 0) for piece in pieces] + [after]
        both = [
            jnp.where(low_edge, down[r], down[r + 1]) + jnp.where(high_edge, up[r + 1], up[r])
            for r in range(len(pieces))
        ]
        return jnp.concatenate(both, 0)

    def split(value, rows, cut, high, low):
        top = value.astype(BF16)
        high[rows, cut] = top
        low[rows, cut] = (value - top.astype(F32)).astype(BF16)

    def solve(place, high, low):
        _, _, first, last, which = place
        top, rest = w_refs[2 * which][...], w_refs[2 * which + 1][...]
        left = high[:, first:last]
        fields = jnp.concatenate([left, low[:, first:last], left], 1)
        return jnp.dot(fields, jnp.concatenate([top, top, rest], 0), preferred_element_type=F32)

    def inside(t, now, later):
        def stencil(cut):
            above, here = u[now, 0, :, cut], u[now, 1, :, cut]
            for a in range(1, na - 1):
                below = u[now, a + 1, :, cut]
                beside = shifted(here, 0.0, 0.0) + (above + below)
                value = ca[a, :, cut] * here + cc[a, :, cut] * beside + cb[a, :, cut]
                split(value, slice((a - 1) * nz, a * nz), cut, xh, xl)
                above, here = here, below

        ready = 0
        for place in places:
            start, stop, _, last, _ = place
            for l in range(ready, last, CHUNK):
                stencil(slice(l, l + CHUNK))
            ready = max(ready, last)
            total = solve(place, xh, xl).reshape(na - 2, nz, stop - start)
            active = jnp.full(total.shape, own_steps, jnp.int32) > t
            u[later, 1 : na - 1, :, start:stop] = jnp.where(active, total, u[now, 1 : na - 1, :, start:stop])

    def border(t, now, later):
        def stencil(cut):
            for n, a, above, below in (
                (0, 0, ha[t, 0, :, cut], u[now, 1, :, cut]),
                (1, na - 1, u[now, na - 2, :, cut], ha[t, 1, :, cut]),
            ):
                here = u[now, a, :, cut]
                outer = hz[t, a : a + 1, cut]
                before, after = jnp.where(ax == 0, 0.0, outer), jnp.where(ax == 0, outer, 0.0)
                beside = shifted(here, before, after) + (above + below)
                value = ca[a, :, cut] * here + cc[a, :, cut] * beside + cb[a, :, cut]
                split(value, slice(n * nz, (n + 1) * nz), cut, bh, bl)
            before, after = (
                jnp.where(ax == 0, ha[t, side, nz - 1 : nz, cut], ha[t, side, 0:1, cut]) for side in (0, 1)
            )
            here = sz[t, :, cut]
            beside = shifted(here, before, after) + (inner[:, cut] + hz[t, :, cut])
            value = fa[:, cut] * here + fc[:, cut] * beside + fb[:, cut]
            split(value, slice(2 * nz, 2 * nz + na), cut, bh, bl)

        ready, arrived = 0, 0
        for place in places:
            start, stop, _, last, _ = place
            cut = slice(start, stop)
            while arrived < len(groups) and groups[arrived][0] < last:
                wait_halo(t, arrived)
                arrived += 1
            for l in range(ready, last, CHUNK):
                stencil(slice(l, l + CHUNK))
            ready = max(ready, last)
            total = solve(place, bh, bl)
            old = jnp.concatenate([u[now, 0, :, cut], u[now, na - 1, :, cut], sz[t, :, cut]], 0)
            total = jnp.where(jnp.full(total.shape, own_steps, jnp.int32) > t, total, old)
            u[later, 0, :, cut] = total[:nz]
            u[later, na - 1, :, cut] = total[nz : 2 * nz]
            sz[t + 1, :, cut] = total[2 * nz :]

            for group, (_, end) in enumerate(groups):
                if end == stop:

                    @pl.when(t < STEPS - 1)
                    def _():
                        send_halo(t + 1, group)

            def scatter(face, near):
                for a in range(1, na - 1):
                    u[later, a, face : face + 1, cut] = sz[t + 1, a : a + 1, cut]

            by_side(scatter)

            @pl.when(t == STEPS - 1)
            def _():
                loop(offsets, start // CHUNK, stop // CHUNK)

    def fine(t, _):
        now, later = lax.rem(t, 2), lax.rem(t + 1, 2)
        inside(t, now, later)
        by_side(lambda face, near: gather(u.at[now], near, inner))
        border(t, now, later)
        return 0

    lax.fori_loop(0, STEPS, fine, 0)

    def pairs(k):
        mate_copy(k).wait()
        cut = lanes_of(k)
        own, theirs = off[ours, :, cut], other[:, :, cut]
        even = jnp.where(core == 0, own, theirs)
        odd = jnp.where(core == 0, theirs, own)
        pair[:, :, cut] = fo[:, :, cut] * even + odd

    def forward(k):
        cut = lanes_of(k)

        @pl.when(chip > 0)
        def _():
            forward_copy(k).wait_recv()

        pout[:, :, cut] = fe[:, :, cut] * fo[:, :, cut] * pin[:, :, cut] + pair[:, :, cut]

        @pl.when(chip < chips - 1)
        def _():
            forward_copy(k).start()

    def backward(k):
        cut = lanes_of(k)

        @pl.when(chip < chips - 1)
        def _():
            backward_copy(k).wait_recv()

        sout[:, :, cut] = fs[:, :, cut] * pair[:, :, cut] + sin[:, :, cut]

        @pl.when(chip > 0)
        def _():
            backward_copy(k).start()

    def settle(k):
        cut = lanes_of(k)
        own, theirs = off[ours, :, cut], other[:, :, cut]
        first = jnp.where(core == 0, own, theirs)
        even = (fp[:, :, cut] * sout[:, :, cut] + pin[:, :, cut]) * inv[:, :, cut]
        odd = fe[:, :, cut] * even + first
        mine[:, :, cut] = jnp.where(core == 0, even, odd)
        give[:, :, cut] = jnp.where(core == 0, odd, even)
        coarse_copy(k).start()
        keep_copy(k).start()

    def send_change(k):
        change_copy(k).start()

    def both(first, second):
        def one(k):
            pairs(k)

            @pl.when(near_odd & (k + AHEAD < chunks))
            def _():
                send_change(k + AHEAD)

            first(k)

            @pl.when(last_odd)
            def _():
                loop(send_change, due(k), due(k + 1))

        def two(k):
            second(k)
            settle(k)

        @pl.when(ends)
        def _():
            loop(one)

            @pl.when((chip == 0) & (core == 1))
            def _():
                loop(send_change)

            @pl.when(last_odd)
            def _():
                loop(send_change, due(chunks), chunks)

            loop(two)

        @pl.when(jnp.logical_not(ends))
        def _():
            loop(one, 0, LAG)

            def step(k):
                one(k)
                two(k - LAG)

            loop(step, LAG, chunks)
            loop(two, chunks - LAG, chunks)

    @pl.when(chip < chips // 2)
    def _():
        both(forward, backward)

    @pl.when(chip >= chips // 2)
    def _():
        both(backward, forward)

    def finish(k):
        keep_copy(k).wait()
        coarse_copy(k).wait()
        change_copy(k).wait()

        @pl.when(chip < chips - 1)
        def _():
            forward_copy(k).wait_send()

        @pl.when(chip > 0)
        def _():
            backward_copy(k).wait_send()

    loop(finish)


def spread(coarse_ref, change_ref, out_ref):
    for r in range(coarse_ref.shape[0]):
        out_ref[0, 2 * r] = coarse_ref[r] + change_ref[r]
        out_ref[0, 2 * r + 1] = coarse_ref[r] - change_ref[r]


def solution(mesh):
    sizes = tuple(mesh.shape[name] for name in ("tm", "ang", "ax"))

    def local(starts, drive, region_ids, steps, reluctivity, resistivity, rates):
        na, nz, rad = region_ids.shape
        half, part = na // 2, na // 4
        blocks, places = inverse_blocks(rad)
        weights = [jnp.asarray(piece) for block in blocks for piece in block]
        smem = pl.BlockSpec(memory_space=pltpu.SMEM)
        anywhere = pl.BlockSpec(memory_space=pltpu.HBM)

        def field(*lead):
            return pltpu.VMEM(lead + (nz, rad), F32)

        halo = pltpu.VMEM((STEPS, 2, nz, rad), F32)
        face = pltpu.VMEM((STEPS, na, rad), F32)
        dma = pltpu.SemaphoreType.DMA
        edge = pltpu.VMEM((na, rad), F32)
        inside = pltpu.VMEM(((na - 2) * nz, rad), BF16)
        border = pltpu.VMEM((2 * nz + na, rad), BF16)
        scratch = [
            field(na), pltpu.VMEM((na, nz, rad), jnp.int32),
            field(2, na), field(na), field(na), field(na), field(half),
            inside, inside, border, border,
            halo, face, pltpu.VMEM((STEPS + 1, na, rad), F32), edge, edge, edge, edge,
            field(half), field(half), field(half), field(part),
        ]
        scratch += [field(part)] * 5 + [field(part)] * 7
        scratch += [dma((STEPS, len(GROUPS) + 1, 2))] * 2 + [dma((STEPS, len(GROUPS) + 1))] * 2 + [dma((rad // CHUNK,))] * 10
        scratch += [dma((3 + len(weights),)), dma((rad // CHUNK,))]
        scratch += [pltpu.VMEM(piece.shape, BF16) for piece in weights]
        pairs = jax.ShapeDtypeStruct((half, nz, rad), F32)
        coarse, change = pl.pallas_call(
            functools.partial(kernel, sizes, places, len(blocks)),
            out_shape=(pairs, pairs),
            in_specs=[smem] * 4 + [anywhere] * (3 + len(weights)),
            out_specs=[pl.BlockSpec(memory_space=pl.ANY)] * 2,
            scratch_shapes=scratch,
            compiler_params=pltpu.CompilerParams(
                collective_id=0, has_side_effects=True, vmem_limit_bytes=VMEM_LIMIT
            ),
        )(steps, reluctivity, resistivity, rates, starts, drive, region_ids, *weights)
        rows = half // SPLIT
        narrow = pl.BlockSpec((rows, nz, rad), lambda i: (i, 0, 0))
        return pl.pallas_call(
            spread,
            grid=(SPLIT,),
            out_shape=jax.ShapeDtypeStruct(starts.shape, F32),
            in_specs=[narrow] * 2,
            out_specs=pl.BlockSpec((1, 2 * rows, nz, rad), lambda i: (0, i, 0, 0)),
        )(coarse, change)

    cells = P("tm", "ang", "ax", None)
    placed = (cells, cells, P("ang", "ax", None), P(), P(), P(), P())
    return jax.shard_map(local, mesh=mesh, in_specs=placed, out_specs=cells, check_vma=False)
```

```python
import functools

import jax
import jax.numpy as jnp
import ml_dtypes
import numpy as np
from jax import lax
from jax.experimental import pallas as pl
from jax.experimental.pallas import tpu as pltpu
from jax.sharding import PartitionSpec as P

STEPS = 4
LANES = 384
WIDE = 256
EDGE = 128
CHUNK = 128
TALL = 8
SPLIT = 2
VMEM_LIMIT = 60 * 2**20
AHEAD = 5
LAG = 5
BURST = 6
RATE = (1, 2)
FRONT = ()

radial_weight = 1.0
explicit_limit = 0.23
F32 = jnp.float32
BF16 = jnp.bfloat16


def inverse_blocks(size):
    middle = 2.0 + 1.0 / radial_weight
    r = (middle - np.sqrt(middle * middle - 4.0)) / 2.0
    index = np.arange(size, dtype=np.float64)
    low = np.minimum(index[:, None], index[None, :])
    high = np.maximum(index[:, None], index[None, :])
    full = r ** (high - low) * (1 - r ** (2 * low + 2)) * (1 - r ** (2 * (size - high)))
    full = full / ((1 / r - r) * (1 - r ** (2 * size + 2)) * radial_weight)
    full = full.astype(np.float32)
    blocks, places, seen = [], [], {}
    starts = [0, *range(size % WIDE or WIDE, size, WIDE)]
    for start, stop in zip(starts, starts[1:] + [size]):
        first, last = max(start - EDGE, 0), min(stop + EDGE, size)
        block = np.ascontiguousarray(full[first:last, start:stop])
        key = (block.shape, block.tobytes())
        if key not in seen:
            seen[key] = len(blocks)
            top = block.astype(ml_dtypes.bfloat16)
            rest = (block - top.astype(np.float32)).astype(ml_dtypes.bfloat16)
            blocks.append((top, rest))
        places.append((start, stop, first, last, seen[key]))
    return blocks, places


def send_groups(places):
    cuts = sorted({0, *FRONT, *(stop for _, stop, *_ in places)})
    return list(zip(cuts, cuts[1:]))


def kernel(sizes, places, nblocks, *refs):
    tm_count, ang_count, ax_count = sizes
    steps_ref, reluct_ref, resist_ref, rates_ref, s_hbm, q_hbm, ids_hbm = refs[:7]
    w_hbm = refs[7 : 7 + 2 * nblocks]
    coarse_ref, rdif = refs[7 + 2 * nblocks : 9 + 2 * nblocks]
    (
        q_ref, ids_ref, u, ca, cc, cb, rc, xh, xl, bh, bl, ha, hz, sa, sz, inner, fa, fc, fb,
        gs, off, dif, other, fs, fp, inv, fe, fo,
        pair, pin, sin, pout, sout, mine, give,
        a_send, a_recv, z_send, z_recv, o_send, o_recv,
        d_send, d_recv, p_send, p_recv, q_send, q_recv, c_send, c_recv, in_sem, out_sem, *w_refs
    ) = refs[9 + 2 * nblocks :]
    na, nz, rad = ids_ref.shape
    half = na // 2
    part = half // 2
    regions = rates_ref.shape[0]
    tm, ang, ax = lax.axis_index("tm"), lax.axis_index("ang"), lax.axis_index("ax")
    core, chip = lax.rem(tm, 2), tm // 2
    chips = tm_count // 2
    mate = tm + 1 - 2 * core

    def ring(value, step, count):
        return lax.rem(value + step + count, count)

    loads = [(s_hbm.at[0], u.at[0]), (ids_hbm, ids_ref), (q_hbm.at[0], q_ref), *zip(w_hbm, w_refs)]
    loads = [pltpu.make_async_copy(a, b, in_sem.at[n]) for n, (a, b) in enumerate(loads)]
    barrier = pltpu.get_barrier_semaphore()
    greet = [("ang", ang, 1, ang_count), ("ang", ang, -1, ang_count)]
    greet += [("ax", ax, 1, ax_count)]
    greet += [("tm", tm, step, tm_count) for step in (1, -1, 2, -2)]
    for axis, value, step, count in greet:
        pl.semaphore_signal(
            barrier, inc=1, device_id={axis: ring(value, step, count)},
            device_id_type=pl.DeviceIdType.MESH,
        )

    for load in loads:
        load.start()

    def remote(src, dst, send, recv, device):
        return pltpu.make_async_remote_copy(
            src_ref=src, dst_ref=dst, send_sem=send, recv_sem=recv,
            device_id=device, device_id_type=pl.DeviceIdType.MESH,
        )

    groups = send_groups(places)

    def ang_copies(t, block):
        lanes = slice(*groups[block])
        if ang_count == 2:
            routes = [(slice(None), 1 - ang)]
        else:
            routes = [(0, ring(ang, 1, ang_count)), (1, ring(ang, -1, ang_count))]
        return [
            remote(
                sa.at[t, side, :, lanes], ha.at[t, side, :, lanes],
                a_send.at[lax.rem(t, 2), block, n], a_recv.at[lax.rem(t, 2), block, n], {"ang": device},
            )
            for n, (side, device) in enumerate(routes)
        ]

    def ax_copy(t, block):
        lanes = slice(*groups[block])
        return remote(
            sz.at[t, :, lanes], hz.at[t, :, lanes],
            z_send.at[lax.rem(t, 2), block], z_recv.at[lax.rem(t, 2), block], {"ax": 1 - ax},
        )

    def send_halo(t, block):
        for copy in ang_copies(t, block):
            copy.start()
        ax_copy(t, block).start()

    def wait_halo(t, block):
        for copy in ang_copies(t, block):
            copy.wait()
        ax_copy(t, block).wait()

    def by_side(body):
        @pl.when(ax == 0)
        def _():
            body(nz - 1, nz - 2)

        @pl.when(ax == 1)
        def _():
            body(0, 1)

    def gather(field, face, into):
        for a in range(na):
            into[a : a + 1, :] = field[a, face : face + 1, :]

    @pl.when(chip == 0)
    def _():
        pin[...] = jnp.zeros_like(pin)

    @pl.when(chip == chips - 1)
    def _():
        sin[...] = jnp.zeros_like(sin)

    loads[0].wait()
    sa[0, 0] = u[0, na - 1]
    sa[0, 1] = u[0, 0]
    by_side(lambda face, near: gather(u.at[0], face, sz.at[0]))
    pl.semaphore_wait(barrier, len(greet))
    for block in range(len(groups)):
        send_halo(0, block)

    loads[1].wait()
    loads[2].wait()
    reluct = [explicit_limit * reluct_ref[k] * resist_ref[k] for k in range(regions)]
    rates = [rates_ref[k] for k in range(regions)]
    own_steps = steps_ref[tm]

    def tables(a, _):
        for l in range(0, rad, LANES):
            cut = slice(l, l + LANES)
            ids = ids_ref[a, :, cut]
            coupling = jnp.zeros(ids.shape, F32)
            relax = jnp.zeros(ids.shape, F32)
            for k in range(regions):
                hit = ids == k
                coupling = jnp.where(hit, reluct[k], coupling)
                relax = jnp.where(hit, rates[k], relax)
            cc[a, :, cut] = coupling
            ca[a, :, cut] = 1.0 - 4.0 * coupling - relax
            cb[a, :, cut] = relax * q_ref[a, :, cut]
            previous = rc[a // 2, :, cut]
            rc[a // 2, :, cut] = jnp.where(lax.rem(a, 2) == 0, relax, 0.5 * (previous + relax))
        return 0

    lax.fori_loop(0, na, tables, 0)

    def side_tables(face, near):
        for field, into in ((ca, fa), (cc, fc), (cb, fb)):
            gather(field, face, into)

    by_side(side_tables)

    def own_factor(i, _):
        mean = (u[0, 2 * i] + u[0, 2 * i + 1]) * 0.5
        gs[i] = mean / (1.0 + own_steps.astype(F32) * rc[i])
        return 0

    lax.fori_loop(0, half, own_factor, 0)

    def factors(k, _):
        rate = rc[part * core + k]
        before = jnp.ones_like(rate)
        after = jnp.ones_like(rate)
        for j in range(tm_count):
            count = steps_ref[j].astype(F32)
            before = before * (1.0 + jnp.where(j < 2 * chip, count, 0.0) * rate)
            after = after * (1.0 + jnp.where(j > 2 * chip + 1, count, 0.0) * rate)
        even = 1.0 + steps_ref[2 * chip].astype(F32) * rate
        odd = 1.0 + steps_ref[2 * chip + 1].astype(F32) * rate
        whole = before * after * (even * odd)
        fs[k] = 1.0 / after
        fp[k] = 1.0 / before
        fe[k] = 1.0 / even
        fo[k] = 1.0 / odd
        inv[k] = whole / (whole - 1.0)
        return 0

    lax.fori_loop(0, part, factors, 0)
    for load in loads[3:]:
        load.wait()

    chunks = rad // CHUNK

    def lanes_of(k):
        if k is None:
            return slice(None)
        return pl.ds(pl.multiple_of(k * CHUNK, CHUNK), CHUNK)

    ours, yours = pl.ds(part * core, part), pl.ds(part * (1 - core), part)

    def mate_copy(k):
        cut = lanes_of(k)
        return remote(
            off.at[yours, :, cut], other.at[:, :, cut], o_send.at[0], o_recv.at[0 if k is None else k], {"tm": mate}
        )

    def change_copy(k):
        cut = lanes_of(k)
        return remote(
            dif.at[:, :, cut], rdif.at[:, :, cut], d_send.at[0], d_recv.at[0 if k is None else k],
            {"tm": ring(tm, 1, tm_count)},
        )

    def forward_copy(k):
        cut = lanes_of(k)
        return remote(
            pout.at[:, :, cut], pin.at[:, :, cut], p_send.at[0], p_recv.at[0 if k is None else k],
            {"tm": ring(tm, 2, tm_count)},
        )

    def backward_copy(k):
        cut = lanes_of(k)
        return remote(
            sout.at[:, :, cut], sin.at[:, :, cut], q_send.at[0], q_recv.at[0 if k is None else k],
            {"tm": ring(tm, -2, tm_count)},
        )

    def coarse_copy(k):
        cut = lanes_of(k)
        return remote(
            give.at[:, :, cut], coarse_ref.at[ours, :, cut], c_send.at[0], c_recv.at[0 if k is None else k], {"tm": mate}
        )

    def keep_copy(k):
        cut = lanes_of(k)
        return pltpu.make_async_copy(mine.at[:, :, cut], coarse_ref.at[ours, :, cut], out_sem.at[0])

    def loop(body, first=0, last=chunks):
        def step(k, _):
            body(k)
            return 0

        lax.fori_loop(first, last, step, 0)

    ends = (chip == 0) | (chip == chips - 1)
    near_odd = jnp.logical_not(ends) & (core == 1)
    last_odd = (chip == chips - 1) & (core == 1)

    def due(k):
        return jnp.minimum(BURST + k * RATE[0] // RATE[1], chunks)

    def offsets(k):
        cut = lanes_of(k)
        for i in range(half):
            even, odd = u[STEPS % 2, 2 * i, :, cut], u[STEPS % 2, 2 * i + 1, :, cut]
            off[i, :, cut] = (even + odd) * 0.5 - gs[i, :, cut]
            dif[i, :, cut] = (even - odd) * 0.5
        mate_copy(k).start()

        soon = (core == 0) | (near_odd & (k < AHEAD)) | (last_odd & (k < BURST))

        @pl.when(soon)
        def _():
            change_copy(k).start()

    spot = lax.broadcasted_iota(jnp.int32, (TALL, CHUNK), 0)
    low_edge, high_edge = spot == 0, spot == TALL - 1

    def shifted(here, before, after):
        pieces = [here[r : r + TALL] for r in range(0, here.shape[0], TALL)]
        down = [before] + [pltpu.roll(piece, 1, 0) for piece in pieces]
        up = [pltpu.roll(piece, TALL - 1, 0) for piece in pieces] + [after]
        both = [
            jnp.where(low_edge, down[r], down[r + 1]) + jnp.where(high_edge, up[r + 1], up[r])
            for r in range(len(pieces))
        ]
        return jnp.concatenate(both, 0)

    def split(value, rows, cut, high, low):
        top = value.astype(BF16)
        high[rows, cut] = top
        low[rows, cut] = (value - top.astype(F32)).astype(BF16)

    def solve(place, high, low):
        _, _, first, last, which = place
        top, rest = w_refs[2 * which][...], w_refs[2 * which + 1][...]
        left = high[:, first:last]
        fields = jnp.concatenate([left, low[:, first:last], left], 1)
        return jnp.dot(fields, jnp.concatenate([top, top, rest], 0), preferred_element_type=F32)

    def inside(t, now, later):
        def stencil(cut):
            above, here = u[now, 0, :, cut], u[now, 1, :, cut]
            for a in range(1, na - 1):
                below = u[now, a + 1, :, cut]
                beside = shifted(here, 0.0, 0.0) + (above + below)
                value = ca[a, :, cut] * here + cc[a, :, cut] * beside + cb[a, :, cut]
                split(value, slice((a - 1) * nz, a * nz), cut, xh, xl)
                above, here = here, below

        ready = 0
        for place in places:
            start, stop, _, last, _ = place
            for l in range(ready, last, CHUNK):
                stencil(slice(l, l + CHUNK))
            ready = max(ready, last)
            total = solve(place, xh, xl).reshape(na - 2, nz, stop - start)
            active = jnp.full(total.shape, own_steps, jnp.int32) > t
            u[later, 1 : na - 1, :, start:stop] = jnp.where(active, total, u[now, 1 : na - 1, :, start:stop])

    def scatter(t, later, cut, face, near):
        for a in range(1, na - 1):
            u[later, a, face : face + 1, cut] = sz[t + 1, a : a + 1, cut]

    def border(t, now, later):
        def stencil(cut):
            for n, a, above, below in (
                (0, 0, ha[t, 0, :, cut], u[now, 1, :, cut]),
                (1, na - 1, u[now, na - 2, :, cut], ha[t, 1, :, cut]),
            ):
                here = u[now, a, :, cut]
                outer = hz[t, a : a + 1, cut]
                before, after = jnp.where(ax == 0, 0.0, outer), jnp.where(ax == 0, outer, 0.0)
                beside = shifted(here, before, after) + (above + below)
                value = ca[a, :, cut] * here + cc[a, :, cut] * beside + cb[a, :, cut]
                split(value, slice(n * nz, (n + 1) * nz), cut, bh, bl)
            before, after = (
                jnp.where(ax == 0, ha[t, side, nz - 1 : nz, cut], ha[t, side, 0:1, cut]) for side in (0, 1)
            )
            here = sz[t, :, cut]
            beside = shifted(here, before, after) + (inner[:, cut] + hz[t, :, cut])
            value = fa[:, cut] * here + fc[:, cut] * beside + fb[:, cut]
            split(value, slice(2 * nz, 2 * nz + na), cut, bh, bl)

        ready, arrived = 0, 0
        for place in places:
            start, stop, _, last, _ = place
            cut = slice(start, stop)
            while arrived < len(groups) and groups[arrived][0] < last:
                wait_halo(t, arrived)
                arrived += 1
            for l in range(ready, last, CHUNK):
                stencil(slice(l, l + CHUNK))
            ready = max(ready, last)
            total = solve(place, bh, bl)
            old = jnp.concatenate([u[now, 0, :, cut], u[now, na - 1, :, cut], sz[t, :, cut]], 0)
            total = jnp.where(jnp.full(total.shape, own_steps, jnp.int32) > t, total, old)
            u[later, 0, :, cut] = total[:nz]
            u[later, na - 1, :, cut] = total[nz : 2 * nz]
            sa[t + 1, 1, :, cut] = total[:nz]
            sa[t + 1, 0, :, cut] = total[nz : 2 * nz]
            sz[t + 1, :, cut] = total[2 * nz :]

            @pl.when(t < STEPS - 1)
            def _():
                for group, (begin, _) in enumerate(groups):
                    if start <= begin < stop:
                        send_halo(t + 1, group)

            @pl.when(t == STEPS - 1)
            def _():
                by_side(functools.partial(scatter, t, later, cut))
                loop(offsets, start // CHUNK, stop // CHUNK)

    def fine(t, _):
        now, later = lax.rem(t, 2), lax.rem(t + 1, 2)
        inside(t, now, later)
        border(t, now, later)

        def ready(face, near):
            scatter(t, later, slice(None), face, near)
            gather(u.at[later], near, inner)

        @pl.when(t < STEPS - 1)
        def _():
            by_side(ready)

        return 0

    by_side(lambda face, near: gather(u.at[0], near, inner))
    lax.fori_loop(0, STEPS, fine, 0)

    def pairs(k):
        mate_copy(k).wait_recv()
        cut = lanes_of(k)
        own, theirs = off[ours, :, cut], other[:, :, cut]
        even = jnp.where(core == 0, own, theirs)
        odd = jnp.where(core == 0, theirs, own)
        pair[:, :, cut] = fo[:, :, cut] * even + odd

    def forward(k):
        cut = lanes_of(k)

        @pl.when(chip > 0)
        def _():
            forward_copy(k).wait_recv()

        pout[:, :, cut] = fe[:, :, cut] * fo[:, :, cut] * pin[:, :, cut] + pair[:, :, cut]

        @pl.when(chip < chips - 1)
        def _():
            forward_copy(k).start()

    def backward(k):
        cut = lanes_of(k)

        @pl.when(chip < chips - 1)
        def _():
            backward_copy(k).wait_recv()

        sout[:, :, cut] = fs[:, :, cut] * pair[:, :, cut] + sin[:, :, cut]

        @pl.when(chip > 0)
        def _():
            backward_copy(k).start()

    def settle(k):
        cut = lanes_of(k)
        own, theirs = off[ours, :, cut], other[:, :, cut]
        first = jnp.where(core == 0, own, theirs)
        even = (fp[:, :, cut] * sout[:, :, cut] + pin[:, :, cut]) * inv[:, :, cut]
        odd = fe[:, :, cut] * even + first
        mine[:, :, cut] = jnp.where(core == 0, even, odd)
        give[:, :, cut] = jnp.where(core == 0, odd, even)
        coarse_copy(k).start()
        keep_copy(k).start()

    def send_change(k):
        change_copy(k).start()

    def both(first, second):
        def one(k):
            pairs(k)
            first(k)

            @pl.when(last_odd)
            def _():
                loop(send_change, due(k), due(k + 1))

        def relay(k):
            first(k)

            @pl.when(near_odd & (k + AHEAD < chunks))
            def _():
                send_change(k + AHEAD)

        def two(k):
            second(k)
            settle(k)

        @pl.when(ends)
        def _():
            loop(one)

            @pl.when((chip == 0) & (core == 1))
            def _():
                loop(send_change)

            @pl.when(last_odd)
            def _():
                loop(send_change, due(chunks), chunks)

            loop(two)

        @pl.when(jnp.logical_not(ends))
        def _():
            loop(pairs)
            loop(relay, 0, LAG)

            def step(k):
                relay(k)
                two(k - LAG)

            loop(step, LAG, chunks)
            loop(two, chunks - LAG, chunks)

    @pl.when(chip < chips // 2)
    def _():
        both(forward, backward)

    @pl.when(chip >= chips // 2)
    def _():
        both(backward, forward)

    def finish(k):
        coarse_copy(k).wait_recv()
        change_copy(k).wait_recv()

    loop(finish)
    keep_copy(None).wait()
    for copy in (mate_copy, coarse_copy, change_copy):
        copy(None).wait_send()

    @pl.when(chip < chips - 1)
    def _():
        forward_copy(None).wait_send()

    @pl.when(chip > 0)
    def _():
        backward_copy(None).wait_send()


def spread(coarse_ref, change_ref, out_ref):
    for r in range(coarse_ref.shape[0]):
        out_ref[0, 2 * r] = coarse_ref[r] + change_ref[r]
        out_ref[0, 2 * r + 1] = coarse_ref[r] - change_ref[r]


def solution(mesh):
    sizes = tuple(mesh.shape[name] for name in ("tm", "ang", "ax"))

    def local(starts, drive, region_ids, steps, reluctivity, resistivity, rates):
        na, nz, rad = region_ids.shape
        half, part = na // 2, na // 4
        blocks, places = inverse_blocks(rad)
        weights = [jnp.asarray(piece) for block in blocks for piece in block]
        smem = pl.BlockSpec(memory_space=pltpu.SMEM)
        anywhere = pl.BlockSpec(memory_space=pltpu.HBM)

        def field(*lead):
            return pltpu.VMEM(lead + (nz, rad), F32)

        halo = pltpu.VMEM((STEPS, 2, nz, rad), F32)
        face = pltpu.VMEM((STEPS, na, rad), F32)
        dma = pltpu.SemaphoreType.DMA
        edge = pltpu.VMEM((na, rad), F32)
        inside = pltpu.VMEM(((na - 2) * nz, rad), BF16)
        border = pltpu.VMEM((2 * nz + na, rad), BF16)
        scratch = [
            field(na), pltpu.VMEM((na, nz, rad), jnp.int32),
            field(2, na), field(na), field(na), field(na), field(half),
            inside, inside, border, border,
            halo, face, pltpu.VMEM((STEPS + 1, 2, nz, rad), F32), pltpu.VMEM((STEPS + 1, na, rad), F32), edge, edge, edge, edge,
            field(half), field(half), field(half), field(part),
        ]
        scratch += [field(part)] * 5 + [field(part)] * 7
        count = len(send_groups(places))
        scratch += [dma((2, count, 1 if sizes[1] == 2 else 2))] * 2 + [dma((2, count))] * 2 + [dma((1,)), dma((rad // CHUNK,))] * 5
        scratch += [dma((3 + len(weights),)), dma((1,))]
        scratch += [pltpu.VMEM(piece.shape, BF16) for piece in weights]
        pairs = jax.ShapeDtypeStruct((half, nz, rad), F32)
        coarse, change = pl.pallas_call(
            functools.partial(kernel, sizes, places, len(blocks)),
            out_shape=(pairs, pairs),
            in_specs=[smem] * 4 + [anywhere] * (3 + len(weights)),
            out_specs=[pl.BlockSpec(memory_space=pl.ANY)] * 2,
            scratch_shapes=scratch,
            compiler_params=pltpu.CompilerParams(
                collective_id=0, has_side_effects=True, vmem_limit_bytes=VMEM_LIMIT
            ),
        )(steps, reluctivity, resistivity, rates, starts, drive, region_ids, *weights)
        rows = half // SPLIT
        narrow = pl.BlockSpec((rows, nz, rad), lambda i: (i, 0, 0))
        return pl.pallas_call(
            spread,
            grid=(SPLIT,),
            out_shape=jax.ShapeDtypeStruct(starts.shape, F32),
            in_specs=[narrow] * 2,
            out_specs=pl.BlockSpec((1, 2 * rows, nz, rad), lambda i: (0, i, 0, 0)),
        )(coarse, change)

    cells = P("tm", "ang", "ax", None)
    placed = (cells, cells, P("ang", "ax", None), P(), P(), P(), P())
    return jax.shard_map(local, mesh=mesh, in_specs=placed, out_specs=cells, check_vma=False)
```

```python
import functools

import jax
import jax.numpy as jnp
import ml_dtypes
import numpy as np
from jax import lax
from jax.experimental import pallas as pl
from jax.experimental.pallas import tpu as pltpu
from jax.sharding import PartitionSpec as P

STEPS = 4
LANES = 384
WIDE = 256
EDGE = 128
CHUNK = 128
TALL = 8
SPLIT = 2
VMEM_LIMIT = 60 * 2**20
AHEAD = 5
LAG = 5
BURST = 6
RATE = (1, 2)
FRONT = ()

radial_weight = 1.0
explicit_limit = 0.23
F32 = jnp.float32
BF16 = jnp.bfloat16


def inverse_blocks(size):
    middle = 2.0 + 1.0 / radial_weight
    r = (middle - np.sqrt(middle * middle - 4.0)) / 2.0
    index = np.arange(size, dtype=np.float64)
    low = np.minimum(index[:, None], index[None, :])
    high = np.maximum(index[:, None], index[None, :])
    full = r ** (high - low) * (1 - r ** (2 * low + 2)) * (1 - r ** (2 * (size - high)))
    full = full / ((1 / r - r) * (1 - r ** (2 * size + 2)) * radial_weight)
    full = full.astype(np.float32)
    blocks, places, seen = [], [], {}
    starts = [0, *range(size % WIDE or WIDE, size, WIDE)]
    for start, stop in zip(starts, starts[1:] + [size]):
        first, last = max(start - EDGE, 0), min(stop + EDGE, size)
        block = np.ascontiguousarray(full[first:last, start:stop])
        key = (block.shape, block.tobytes())
        if key not in seen:
            seen[key] = len(blocks)
            top = block.astype(ml_dtypes.bfloat16)
            rest = (block - top.astype(np.float32)).astype(ml_dtypes.bfloat16)
            blocks.append((top, rest))
        places.append((start, stop, first, last, seen[key]))
    return blocks, places


def send_groups(places):
    cuts = sorted({0, *FRONT, *(stop for _, stop, *_ in places)})
    return list(zip(cuts, cuts[1:]))


def kernel(sizes, places, depths, *refs):
    nblocks = len(depths)
    tm_count, ang_count, ax_count = sizes
    steps_ref, reluct_ref, resist_ref, rates_ref, s_hbm, q_hbm, ids_hbm = refs[:7]
    w_hbm, coarse_ref, rdif = refs[7:10]
    (
        q_ref, ids_ref, u, ca, cc, cb, rc, xh, xl, bh, bl, ha, hz, sa, sz, inner, fa, fc, fb,
        gs, off, dif, other, fs, fp, inv, fe, fo,
        pair, pin, sin, pout, sout, mine, give,
        a_send, a_recv, z_send, z_recv, o_send, o_recv,
        d_send, d_recv, p_send, p_recv, q_send, q_recv, c_send, c_recv, in_sem, out_sem, w_all
    ) = refs[10:]
    na, nz, rad = ids_ref.shape
    wedges = dict(zip(range(nblocks), np.cumsum([0, *depths])))
    half = na // 2
    part = half // 2
    regions = rates_ref.shape[0]
    tm, ang, ax = lax.axis_index("tm"), lax.axis_index("ang"), lax.axis_index("ax")
    core, chip = lax.rem(tm, 2), tm // 2
    chips = tm_count // 2
    mate = tm + 1 - 2 * core

    def ring(value, step, count):
        return lax.rem(value + step + count, count)

    loads = [(s_hbm.at[0], u.at[0]), (ids_hbm, ids_ref), (q_hbm.at[0], q_ref), (w_hbm, w_all)]
    loads = [pltpu.make_async_copy(a, b, in_sem.at[n]) for n, (a, b) in enumerate(loads)]
    barrier = pltpu.get_barrier_semaphore()
    greet = [("ang", ang, 1, ang_count), ("ang", ang, -1, ang_count)]
    greet += [("ax", ax, 1, ax_count)]
    greet += [("tm", tm, step, tm_count) for step in (1, -1, 2, -2)]
    for axis, value, step, count in greet:
        pl.semaphore_signal(
            barrier, inc=1, device_id={axis: ring(value, step, count)},
            device_id_type=pl.DeviceIdType.MESH,
        )

    for load in loads:
        load.start()

    def remote(src, dst, send, recv, device):
        return pltpu.make_async_remote_copy(
            src_ref=src, dst_ref=dst, send_sem=send, recv_sem=recv,
            device_id=device, device_id_type=pl.DeviceIdType.MESH,
        )

    groups = send_groups(places)

    def ang_copies(t, block):
        lanes = slice(*groups[block])
        if ang_count == 2:
            routes = [(slice(None), 1 - ang)]
        else:
            routes = [(0, ring(ang, 1, ang_count)), (1, ring(ang, -1, ang_count))]
        return [
            remote(
                sa.at[t, side, :, lanes], ha.at[t, side, :, lanes],
                a_send.at[lax.rem(t, 2), block, n], a_recv.at[lax.rem(t, 2), block, n], {"ang": device},
            )
            for n, (side, device) in enumerate(routes)
        ]

    def ax_copy(t, block):
        lanes = slice(*groups[block])
        return remote(
            sz.at[t, :, lanes], hz.at[t, :, lanes],
            z_send.at[lax.rem(t, 2), block], z_recv.at[lax.rem(t, 2), block], {"ax": 1 - ax},
        )

    def send_halo(t, block):
        for copy in ang_copies(t, block):
            copy.start()
        ax_copy(t, block).start()

    def wait_halo(t, block):
        for copy in ang_copies(t, block):
            copy.wait()
        ax_copy(t, block).wait()

    def by_side(body):
        @pl.when(ax == 0)
        def _():
            body(nz - 1, nz - 2)

        @pl.when(ax == 1)
        def _():
            body(0, 1)

    def gather(field, face, into):
        for a in range(na):
            into[a : a + 1, :] = field[a, face : face + 1, :]

    @pl.when(chip == 0)
    def _():
        pin[...] = jnp.zeros_like(pin)

    @pl.when(chip == chips - 1)
    def _():
        sin[...] = jnp.zeros_like(sin)

    loads[0].wait()
    sa[0, 0] = u[0, na - 1]
    sa[0, 1] = u[0, 0]
    by_side(lambda face, near: gather(u.at[0], face, sz.at[0]))
    pl.semaphore_wait(barrier, len(greet))
    for block in range(len(groups)):
        send_halo(0, block)

    loads[1].wait()
    loads[2].wait()
    reluct = [explicit_limit * reluct_ref[k] * resist_ref[k] for k in range(regions)]
    rates = [rates_ref[k] for k in range(regions)]
    own_steps = steps_ref[tm]

    def tables(a, _):
        for l in range(0, rad, LANES):
            cut = slice(l, l + LANES)
            ids = ids_ref[a, :, cut]
            coupling = jnp.zeros(ids.shape, F32)
            relax = jnp.zeros(ids.shape, F32)
            for k in range(regions):
                hit = ids == k
                coupling = jnp.where(hit, reluct[k], coupling)
                relax = jnp.where(hit, rates[k], relax)
            cc[a, :, cut] = coupling
            ca[a, :, cut] = 1.0 - 4.0 * coupling - relax
            cb[a, :, cut] = relax * q_ref[a, :, cut]
            previous = rc[a // 2, :, cut]
            rc[a // 2, :, cut] = jnp.where(lax.rem(a, 2) == 0, relax, 0.5 * (previous + relax))
        return 0

    lax.fori_loop(0, na, tables, 0)

    def side_tables(face, near):
        for field, into in ((ca, fa), (cc, fc), (cb, fb)):
            gather(field, face, into)

    by_side(side_tables)

    def own_factor(i, _):
        mean = (u[0, 2 * i] + u[0, 2 * i + 1]) * 0.5
        gs[i] = mean / (1.0 + own_steps.astype(F32) * rc[i])
        return 0

    lax.fori_loop(0, half, own_factor, 0)

    def factors(k, _):
        rate = rc[part * core + k]
        before = jnp.ones_like(rate)
        after = jnp.ones_like(rate)
        for j in range(tm_count):
            count = steps_ref[j].astype(F32)
            before = before * (1.0 + jnp.where(j < 2 * chip, count, 0.0) * rate)
            after = after * (1.0 + jnp.where(j > 2 * chip + 1, count, 0.0) * rate)
        even = 1.0 + steps_ref[2 * chip].astype(F32) * rate
        odd = 1.0 + steps_ref[2 * chip + 1].astype(F32) * rate
        whole = before * after * (even * odd)
        fs[k] = 1.0 / after
        fp[k] = 1.0 / before
        fe[k] = 1.0 / even
        fo[k] = 1.0 / odd
        inv[k] = whole / (whole - 1.0)
        return 0

    lax.fori_loop(0, part, factors, 0)
    for load in loads[3:]:
        load.wait()

    chunks = rad // CHUNK

    def lanes_of(k):
        if k is None:
            return slice(None)
        return pl.ds(pl.multiple_of(k * CHUNK, CHUNK), CHUNK)

    ours, yours = pl.ds(part * core, part), pl.ds(part * (1 - core), part)

    def mate_copy(k):
        cut = lanes_of(k)
        return remote(
            off.at[yours, :, cut], other.at[:, :, cut], o_send.at[0], o_recv.at[0 if k is None else k], {"tm": mate}
        )

    def change_copy(k):
        cut = lanes_of(k)
        return remote(
            dif.at[:, :, cut], rdif.at[:, :, cut], d_send.at[0], d_recv.at[0],
            {"tm": ring(tm, 1, tm_count)},
        )

    def forward_copy(k):
        cut = lanes_of(k)
        return remote(
            pout.at[:, :, cut], pin.at[:, :, cut], p_send.at[0], p_recv.at[0 if k is None else k],
            {"tm": ring(tm, 2, tm_count)},
        )

    def backward_copy(k):
        cut = lanes_of(k)
        return remote(
            sout.at[:, :, cut], sin.at[:, :, cut], q_send.at[0], q_recv.at[0 if k is None else k],
            {"tm": ring(tm, -2, tm_count)},
        )

    def coarse_copy(k):
        cut = lanes_of(k)
        return remote(
            give.at[:, :, cut], coarse_ref.at[ours, :, cut], c_send.at[0], c_recv.at[0], {"tm": mate}
        )

    def keep_copy(k):
        cut = lanes_of(k)
        return pltpu.make_async_copy(mine.at[:, :, cut], coarse_ref.at[ours, :, cut], out_sem.at[0])

    def loop(body, first=0, last=chunks):
        def step(k, _):
            body(k)
            return 0

        lax.fori_loop(first, last, step, 0)

    ends = (chip == 0) | (chip == chips - 1)
    near_odd = jnp.logical_not(ends) & (core == 1)
    last_odd = (chip == chips - 1) & (core == 1)

    def due(k):
        return jnp.minimum(BURST + k * RATE[0] // RATE[1], chunks)

    def offsets(k):
        cut = lanes_of(k)
        for i in range(half):
            even, odd = u[STEPS % 2, 2 * i, :, cut], u[STEPS % 2, 2 * i + 1, :, cut]
            off[i, :, cut] = (even + odd) * 0.5 - gs[i, :, cut]
            dif[i, :, cut] = (even - odd) * 0.5
        mate_copy(k).start()

        soon = (core == 0) | (near_odd & (k < AHEAD)) | (last_odd & (k < BURST))

        @pl.when(soon)
        def _():
            change_copy(k).start()

    spot = lax.broadcasted_iota(jnp.int32, (TALL, CHUNK), 0)
    low_edge, high_edge = spot == 0, spot == TALL - 1

    def shifted(here, before, after):
        pieces = [here[r : r + TALL] for r in range(0, here.shape[0], TALL)]
        down = [before] + [pltpu.roll(piece, 1, 0) for piece in pieces]
        up = [pltpu.roll(piece, TALL - 1, 0) for piece in pieces] + [after]
        both = [
            jnp.where(low_edge, down[r], down[r + 1]) + jnp.where(high_edge, up[r + 1], up[r])
            for r in range(len(pieces))
        ]
        return jnp.concatenate(both, 0)

    def split(value, rows, cut, high, low):
        top = value.astype(BF16)
        high[rows, cut] = top
        low[rows, cut] = (value - top.astype(F32)).astype(BF16)

    def solve(place, high, low):
        start, stop, first, last, which = place
        row, deep, wide = 2 * wedges[which], last - first, stop - start
        top, rest = w_all[row : row + deep, :wide], w_all[row + deep : row + 2 * deep, :wide]
        left = high[:, first:last]
        fields = jnp.concatenate([left, low[:, first:last], left], 1)
        return jnp.dot(fields, jnp.concatenate([top, top, rest], 0), preferred_element_type=F32)

    def inside(t, now, later):
        def stencil(cut):
            above, here = u[now, 0, :, cut], u[now, 1, :, cut]
            for a in range(1, na - 1):
                below = u[now, a + 1, :, cut]
                beside = shifted(here, 0.0, 0.0) + (above + below)
                value = ca[a, :, cut] * here + cc[a, :, cut] * beside + cb[a, :, cut]
                split(value, slice((a - 1) * nz, a * nz), cut, xh, xl)
                above, here = here, below

        ready = 0
        for place in places:
            start, stop, _, last, _ = place
            for l in range(ready, last, CHUNK):
                stencil(slice(l, l + CHUNK))
            ready = max(ready, last)
            total = solve(place, xh, xl).reshape(na - 2, nz, stop - start)
            active = jnp.full(total.shape, own_steps, jnp.int32) > t
            u[later, 1 : na - 1, :, start:stop] = jnp.where(active, total, u[now, 1 : na - 1, :, start:stop])

    def scatter(t, later, cut, face, near):
        for a in range(1, na - 1):
            u[later, a, face : face + 1, cut] = sz[t + 1, a : a + 1, cut]

    def border(t, now, later):
        def stencil(cut):
            for n, a, above, below in (
                (0, 0, ha[t, 0, :, cut], u[now, 1, :, cut]),
                (1, na - 1, u[now, na - 2, :, cut], ha[t, 1, :, cut]),
            ):
                here = u[now, a, :, cut]
                outer = hz[t, a : a + 1, cut]
                before, after = jnp.where(ax == 0, 0.0, outer), jnp.where(ax == 0, outer, 0.0)
                beside = shifted(here, before, after) + (above + below)
                value = ca[a, :, cut] * here + cc[a, :, cut] * beside + cb[a, :, cut]
                split(value, slice(n * nz, (n + 1) * nz), cut, bh, bl)
            before, after = (
                jnp.where(ax == 0, ha[t, side, nz - 1 : nz, cut], ha[t, side, 0:1, cut]) for side in (0, 1)
            )
            here = sz[t, :, cut]
            beside = shifted(here, before, after) + (inner[:, cut] + hz[t, :, cut])
            value = fa[:, cut] * here + fc[:, cut] * beside + fb[:, cut]
            split(value, slice(2 * nz, 2 * nz + na), cut, bh, bl)

        ready, arrived = 0, 0
        for place in places:
            start, stop, _, last, _ = place
            cut = slice(start, stop)
            while arrived < len(groups) and groups[arrived][0] < last:
                wait_halo(t, arrived)
                arrived += 1
            for l in range(ready, last, CHUNK):
                stencil(slice(l, l + CHUNK))
            ready = max(ready, last)
            total = solve(place, bh, bl)
            old = jnp.concatenate([u[now, 0, :, cut], u[now, na - 1, :, cut], sz[t, :, cut]], 0)
            total = jnp.where(jnp.full(total.shape, own_steps, jnp.int32) > t, total, old)
            u[later, 0, :, cut] = total[:nz]
            u[later, na - 1, :, cut] = total[nz : 2 * nz]
            sa[t + 1, 1, :, cut] = total[:nz]
            sa[t + 1, 0, :, cut] = total[nz : 2 * nz]
            sz[t + 1, :, cut] = total[2 * nz :]

            @pl.when(t < STEPS - 1)
            def _():
                for group, (begin, _) in enumerate(groups):
                    if start <= begin < stop:
                        send_halo(t + 1, group)

            @pl.when(t == STEPS - 1)
            def _():
                by_side(functools.partial(scatter, t, later, cut))
                loop(offsets, start // CHUNK, stop // CHUNK)

    def fine(t, _):
        now, later = lax.rem(t, 2), lax.rem(t + 1, 2)
        inside(t, now, later)
        border(t, now, later)

        def ready(face, near):
            scatter(t, later, slice(None), face, near)
            gather(u.at[later], near, inner)

        @pl.when(t < STEPS - 1)
        def _():
            by_side(ready)

        return 0

    by_side(lambda face, near: gather(u.at[0], near, inner))
    lax.fori_loop(0, STEPS, fine, 0)

    def pairs(k):
        mate_copy(k).wait_recv()
        cut = lanes_of(k)
        own, theirs = off[ours, :, cut], other[:, :, cut]
        even = jnp.where(core == 0, own, theirs)
        odd = jnp.where(core == 0, theirs, own)
        pair[:, :, cut] = fo[:, :, cut] * even + odd

    def forward(k):
        cut = lanes_of(k)

        @pl.when(chip > 0)
        def _():
            forward_copy(k).wait_recv()

        pout[:, :, cut] = fe[:, :, cut] * fo[:, :, cut] * pin[:, :, cut] + pair[:, :, cut]

        @pl.when(chip < chips - 1)
        def _():
            forward_copy(k).start()

    def backward(k):
        cut = lanes_of(k)

        @pl.when(chip < chips - 1)
        def _():
            backward_copy(k).wait_recv()

        sout[:, :, cut] = fs[:, :, cut] * pair[:, :, cut] + sin[:, :, cut]

        @pl.when(chip > 0)
        def _():
            backward_copy(k).start()

    def settle(k):
        cut = lanes_of(k)
        own, theirs = off[ours, :, cut], other[:, :, cut]
        first = jnp.where(core == 0, own, theirs)
        even = (fp[:, :, cut] * sout[:, :, cut] + pin[:, :, cut]) * inv[:, :, cut]
        odd = fe[:, :, cut] * even + first
        mine[:, :, cut] = jnp.where(core == 0, even, odd)
        give[:, :, cut] = jnp.where(core == 0, odd, even)
        coarse_copy(k).start()
        keep_copy(k).start()

    def send_change(k):
        change_copy(k).start()

    def both(first, second):
        def one(k):
            pairs(k)
            first(k)

            @pl.when(last_odd)
            def _():
                loop(send_change, due(k), due(k + 1))

        def relay(k):
            first(k)

            @pl.when(near_odd & (k + AHEAD < chunks))
            def _():
                send_change(k + AHEAD)

        def two(k):
            second(k)
            settle(k)

        @pl.when(ends)
        def _():
            loop(one)

            @pl.when((chip == 0) & (core == 1))
            def _():
                loop(send_change)

            @pl.when(last_odd)
            def _():
                loop(send_change, due(chunks), chunks)

            loop(two)

        @pl.when(jnp.logical_not(ends))
        def _():
            loop(pairs)
            loop(relay, 0, LAG)

            def step(k):
                relay(k)
                two(k - LAG)

            loop(step, LAG, chunks)
            loop(two, chunks - LAG, chunks)

    @pl.when(chip < chips // 2)
    def _():
        both(forward, backward)

    @pl.when(chip >= chips // 2)
    def _():
        both(backward, forward)

    keep_copy(None).wait()
    coarse_copy(None).wait()
    change_copy(None).wait()
    mate_copy(None).wait_send()

    @pl.when(chip < chips - 1)
    def _():
        forward_copy(None).wait_send()

    @pl.when(chip > 0)
    def _():
        backward_copy(None).wait_send()


def spread(coarse_ref, change_ref, out_ref):
    for r in range(coarse_ref.shape[0]):
        out_ref[0, 2 * r] = coarse_ref[r] + change_ref[r]
        out_ref[0, 2 * r + 1] = coarse_ref[r] - change_ref[r]


def solution(mesh):
    sizes = tuple(mesh.shape[name] for name in ("tm", "ang", "ax"))

    def local(starts, drive, region_ids, steps, reluctivity, resistivity, rates):
        na, nz, rad = region_ids.shape
        half, part = na // 2, na // 4
        blocks, places = inverse_blocks(rad)
        weights = np.concatenate(
            [np.pad(piece, ((0, 0), (0, WIDE - piece.shape[1]))) for block in blocks for piece in block]
        )
        smem = pl.BlockSpec(memory_space=pltpu.SMEM)
        anywhere = pl.BlockSpec(memory_space=pltpu.HBM)

        def field(*lead):
            return pltpu.VMEM(lead + (nz, rad), F32)

        halo = pltpu.VMEM((STEPS, 2, nz, rad), F32)
        face = pltpu.VMEM((STEPS, na, rad), F32)
        dma = pltpu.SemaphoreType.DMA
        edge = pltpu.VMEM((na, rad), F32)
        inside = pltpu.VMEM(((na - 2) * nz, rad), BF16)
        border = pltpu.VMEM((2 * nz + na, rad), BF16)
        scratch = [
            field(na), pltpu.VMEM((na, nz, rad), jnp.int32),
            field(2, na), field(na), field(na), field(na), field(half),
            inside, inside, border, border,
            halo, face, pltpu.VMEM((STEPS + 1, 2, nz, rad), F32), pltpu.VMEM((STEPS + 1, na, rad), F32), edge, edge, edge, edge,
            field(half), field(half), field(half), field(part),
        ]
        scratch += [field(part)] * 5 + [field(part)] * 7
        count = len(send_groups(places))
        scratch += [dma((2, count, 1 if sizes[1] == 2 else 2))] * 2 + [dma((2, count))] * 2 + [dma((1,)), dma((rad // CHUNK,)), dma((1,)), dma((1,))]
        scratch += [dma((1,)), dma((rad // CHUNK,))] * 2 + [dma((1,))] * 2
        scratch += [dma((4,)), dma((1,))]
        scratch += [pltpu.VMEM(weights.shape, BF16)]
        pairs = jax.ShapeDtypeStruct((half, nz, rad), F32)
        coarse, change = pl.pallas_call(
            functools.partial(kernel, sizes, places, [top.shape[0] for top, _ in blocks]),
            out_shape=(pairs, pairs),
            in_specs=[smem] * 4 + [anywhere] * 4,
            out_specs=[pl.BlockSpec(memory_space=pl.ANY)] * 2,
            scratch_shapes=scratch,
            compiler_params=pltpu.CompilerParams(
                collective_id=0, has_side_effects=True, vmem_limit_bytes=VMEM_LIMIT
            ),
        )(steps, reluctivity, resistivity, rates, starts, drive, region_ids, jnp.asarray(weights))
        rows = half // SPLIT
        narrow = pl.BlockSpec((rows, nz, rad), lambda i: (i, 0, 0))
        return pl.pallas_call(
            spread,
            grid=(SPLIT,),
            out_shape=jax.ShapeDtypeStruct(starts.shape, F32),
            in_specs=[narrow] * 2,
            out_specs=pl.BlockSpec((1, 2 * rows, nz, rad), lambda i: (0, i, 0, 0)),
        )(coarse, change)

    cells = P("tm", "ang", "ax", None)
    placed = (cells, cells, P("ang", "ax", None), P(), P(), P(), P())
    return jax.shard_map(local, mesh=mesh, in_specs=placed, out_specs=cells, check_vma=False)
```

```python
import functools

import jax
import jax.numpy as jnp
import ml_dtypes
import numpy as np
from jax import lax
from jax.experimental import pallas as pl
from jax.experimental.pallas import tpu as pltpu
from jax.sharding import PartitionSpec as P

STEPS = 4
LANES = 384
WIDE = 256
EDGE = 128
CHUNK = 128
TALL = 8
SPLIT = 2
VMEM_LIMIT = 60 * 2**20
AHEAD = 5
LAG = 5
BURST = 6
RATE = (1, 2)
FRONT = ()

radial_weight = 1.0
explicit_limit = 0.23
F32 = jnp.float32
BF16 = jnp.bfloat16


def inverse_blocks(size):
    middle = 2.0 + 1.0 / radial_weight
    r = (middle - np.sqrt(middle * middle - 4.0)) / 2.0
    index = np.arange(size, dtype=np.float64)
    low = np.minimum(index[:, None], index[None, :])
    high = np.maximum(index[:, None], index[None, :])
    full = r ** (high - low) * (1 - r ** (2 * low + 2)) * (1 - r ** (2 * (size - high)))
    full = full / ((1 / r - r) * (1 - r ** (2 * size + 2)) * radial_weight)
    full = full.astype(np.float32)
    blocks, places, seen = [], [], {}
    starts = [0, *range(size % WIDE or WIDE, size, WIDE)]
    for start, stop in zip(starts, starts[1:] + [size]):
        first, last = max(start - EDGE, 0), min(stop + EDGE, size)
        block = np.ascontiguousarray(full[first:last, start:stop])
        key = (block.shape, block.tobytes())
        if key not in seen:
            seen[key] = len(blocks)
            top = block.astype(ml_dtypes.bfloat16)
            rest = (block - top.astype(np.float32)).astype(ml_dtypes.bfloat16)
            blocks.append((top, rest))
        places.append((start, stop, first, last, seen[key]))
    return blocks, places


def send_groups(places):
    cuts = sorted({0, *FRONT, *(stop for _, stop, *_ in places)})
    return list(zip(cuts, cuts[1:]))


def kernel(sizes, places, depths, *refs):
    nblocks = len(depths)
    tm_count, ang_count, ax_count = sizes
    steps_ref, reluct_ref, resist_ref, rates_ref, s_hbm, q_hbm, ids_hbm = refs[:7]
    w_hbm, coarse_ref, rdif = refs[7:10]
    (
        q_ref, ids_ref, u, ca, cc, cb, rc, xh, xl, bh, bl, ha, hz, sa, sz, inner, fa, fc, fb,
        gs, off, dif, other, fs, fp, inv, fe, fo,
        pair, pin, sin, pout, sout, mine, give,
        a_send, a_recv, z_send, z_recv, o_send, o_recv,
        d_send, d_recv, p_send, p_recv, q_send, q_recv, c_send, c_recv, in_sem, out_sem, w_all
    ) = refs[10:]
    na, nz, rad = ids_ref.shape
    wedges = dict(zip(range(nblocks), np.cumsum([0, *depths])))
    half = na // 2
    part = half // 2
    regions = rates_ref.shape[0]
    tm, ang, ax = lax.axis_index("tm"), lax.axis_index("ang"), lax.axis_index("ax")
    core, chip = lax.rem(tm, 2), tm // 2
    chips = tm_count // 2
    mate = tm + 1 - 2 * core

    def ring(value, step, count):
        return lax.rem(value + step + count, count)

    loads = [(s_hbm.at[0], u.at[0]), (ids_hbm, ids_ref), (q_hbm.at[0], q_ref), (w_hbm, w_all)]
    loads = [pltpu.make_async_copy(a, b, in_sem.at[n]) for n, (a, b) in enumerate(loads)]
    barrier = pltpu.get_barrier_semaphore()
    greet = [("ang", ang, 1, ang_count), ("ang", ang, -1, ang_count)]
    greet += [("ax", ax, 1, ax_count)]
    greet += [("tm", tm, step, tm_count) for step in (1, -1, 2, -2)]
    for axis, value, step, count in greet:
        pl.semaphore_signal(
            barrier, inc=1, device_id={axis: ring(value, step, count)},
            device_id_type=pl.DeviceIdType.MESH,
        )

    for load in loads:
        load.start()

    def remote(src, dst, send, recv, device):
        return pltpu.make_async_remote_copy(
            src_ref=src, dst_ref=dst, send_sem=send, recv_sem=recv,
            device_id=device, device_id_type=pl.DeviceIdType.MESH,
        )

    groups = send_groups(places)

    def ang_copies(t, block):
        lanes = slice(*groups[block])
        if ang_count == 2:
            routes = [(slice(None), 1 - ang)]
        else:
            routes = [(0, ring(ang, 1, ang_count)), (1, ring(ang, -1, ang_count))]
        return [
            remote(
                sa.at[t, side, :, lanes], ha.at[t, side, :, lanes],
                a_send.at[lax.rem(t, 2), block, n], a_recv.at[lax.rem(t, 2), block, n], {"ang": device},
            )
            for n, (side, device) in enumerate(routes)
        ]

    def ax_copy(t, block):
        lanes = slice(*groups[block])
        return remote(
            sz.at[t, :, lanes], hz.at[t, :, lanes],
            z_send.at[lax.rem(t, 2), block], z_recv.at[lax.rem(t, 2), block], {"ax": 1 - ax},
        )

    def send_halo(t, block):
        ax_copy(t, block).start()
        for copy in ang_copies(t, block):
            copy.start()

    def wait_halo(t, block):
        for copy in ang_copies(t, block):
            copy.wait()
        ax_copy(t, block).wait()

    def by_side(body):
        @pl.when(ax == 0)
        def _():
            body(nz - 1, nz - 2)

        @pl.when(ax == 1)
        def _():
            body(0, 1)

    def gather(field, face, into):
        for a in range(na):
            into[a : a + 1, :] = field[a, face : face + 1, :]

    loads[0].wait()
    sa[0, 0] = u[0, na - 1]
    sa[0, 1] = u[0, 0]
    by_side(lambda face, near: gather(u.at[0], face, sz.at[0]))
    pl.semaphore_wait(barrier, len(greet))
    for block in range(len(groups)):
        send_halo(0, block)

    @pl.when(chip == 0)
    def _():
        pin[...] = jnp.zeros_like(pin)

    @pl.when(chip == chips - 1)
    def _():
        sin[...] = jnp.zeros_like(sin)

    loads[1].wait()
    loads[2].wait()
    reluct = [explicit_limit * reluct_ref[k] * resist_ref[k] for k in range(regions)]
    rates = [rates_ref[k] for k in range(regions)]
    own_steps = steps_ref[tm]

    def tables(a, _):
        for l in range(0, rad, LANES):
            cut = slice(l, l + LANES)
            ids = ids_ref[a, :, cut]
            coupling = jnp.zeros(ids.shape, F32)
            relax = jnp.zeros(ids.shape, F32)
            for k in range(regions):
                hit = ids == k
                coupling = jnp.where(hit, reluct[k], coupling)
                relax = jnp.where(hit, rates[k], relax)
            cc[a, :, cut] = coupling
            ca[a, :, cut] = 1.0 - 4.0 * coupling - relax
            cb[a, :, cut] = relax * q_ref[a, :, cut]
            previous = rc[a // 2, :, cut]
            rc[a // 2, :, cut] = jnp.where(lax.rem(a, 2) == 0, relax, 0.5 * (previous + relax))
        return 0

    lax.fori_loop(0, na, tables, 0)

    def side_tables(face, near):
        for field, into in ((ca, fa), (cc, fc), (cb, fb)):
            gather(field, face, into)

    by_side(side_tables)

    def own_factor(i, _):
        mean = (u[0, 2 * i] + u[0, 2 * i + 1]) * 0.5
        gs[i] = mean / (1.0 + own_steps.astype(F32) * rc[i])
        return 0


    def factors(k, _):
        rate = rc[part * core + k]
        before = jnp.ones_like(rate)
        after = jnp.ones_like(rate)
        for j in range(tm_count):
            count = steps_ref[j].astype(F32)
            before = before * (1.0 + jnp.where(j < 2 * chip, count, 0.0) * rate)
            after = after * (1.0 + jnp.where(j > 2 * chip + 1, count, 0.0) * rate)
        even = 1.0 + steps_ref[2 * chip].astype(F32) * rate
        odd = 1.0 + steps_ref[2 * chip + 1].astype(F32) * rate
        whole = before * after * (even * odd)
        fs[k] = 1.0 / after
        fp[k] = 1.0 / before
        fe[k] = 1.0 / even
        fo[k] = 1.0 / odd
        inv[k] = whole / (whole - 1.0)
        return 0

    for load in loads[3:]:
        load.wait()

    chunks = rad // CHUNK

    def lanes_of(k):
        if k is None:
            return slice(None)
        return pl.ds(pl.multiple_of(k * CHUNK, CHUNK), CHUNK)

    ours, yours = pl.ds(part * core, part), pl.ds(part * (1 - core), part)

    def mate_copy(k):
        cut = lanes_of(k)
        return remote(
            off.at[yours, :, cut], other.at[:, :, cut], o_send.at[0], o_recv.at[0 if k is None else k], {"tm": mate}
        )

    def change_copy(k):
        cut = lanes_of(k)
        return remote(
            dif.at[:, :, cut], rdif.at[:, :, cut], d_send.at[0], d_recv.at[0],
            {"tm": ring(tm, 1, tm_count)},
        )

    def forward_copy(k):
        cut = lanes_of(k)
        return remote(
            pout.at[:, :, cut], pin.at[:, :, cut], p_send.at[0], p_recv.at[0 if k is None else k],
            {"tm": ring(tm, 2, tm_count)},
        )

    def backward_copy(k):
        cut = lanes_of(k)
        return remote(
            sout.at[:, :, cut], sin.at[:, :, cut], q_send.at[0], q_recv.at[0 if k is None else k],
            {"tm": ring(tm, -2, tm_count)},
        )

    def coarse_copy(k):
        cut = lanes_of(k)
        return remote(
            give.at[:, :, cut], coarse_ref.at[ours, :, cut], c_send.at[0], c_recv.at[0], {"tm": mate}
        )

    def keep_copy(k):
        cut = lanes_of(k)
        return pltpu.make_async_copy(mine.at[:, :, cut], coarse_ref.at[ours, :, cut], out_sem.at[0])

    def loop(body, first=0, last=chunks):
        def step(k, _):
            body(k)
            return 0

        lax.fori_loop(first, last, step, 0)

    ends = (chip == 0) | (chip == chips - 1)
    near_odd = jnp.logical_not(ends) & (core == 1)
    last_odd = (chip == chips - 1) & (core == 1)

    def due(k):
        return jnp.minimum(BURST + k * RATE[0] // RATE[1], chunks)

    def offsets(k):
        cut = lanes_of(k)
        for i in range(half):
            even, odd = u[STEPS % 2, 2 * i, :, cut], u[STEPS % 2, 2 * i + 1, :, cut]
            off[i, :, cut] = (even + odd) * 0.5 - gs[i, :, cut]
            dif[i, :, cut] = (even - odd) * 0.5
        mate_copy(k).start()

        soon = (core == 0) | (near_odd & (k < AHEAD)) | (last_odd & (k < BURST))

        @pl.when(soon)
        def _():
            change_copy(k).start()

    spot = lax.broadcasted_iota(jnp.int32, (TALL, CHUNK), 0)
    low_edge, high_edge = spot == 0, spot == TALL - 1

    def shifted(here, before, after):
        pieces = [here[r : r + TALL] for r in range(0, here.shape[0], TALL)]
        down = [before] + [pltpu.roll(piece, 1, 0) for piece in pieces]
        up = [pltpu.roll(piece, TALL - 1, 0) for piece in pieces] + [after]
        both = [
            jnp.where(low_edge, down[r], down[r + 1]) + jnp.where(high_edge, up[r + 1], up[r])
            for r in range(len(pieces))
        ]
        return jnp.concatenate(both, 0)

    def split(value, rows, cut, high, low):
        top = value.astype(BF16)
        high[rows, cut] = top
        low[rows, cut] = (value - top.astype(F32)).astype(BF16)

    def solve(place, high, low):
        start, stop, first, last, which = place
        row, deep, wide = 2 * wedges[which], last - first, stop - start
        top, rest = w_all[row : row + deep, :wide], w_all[row + deep : row + 2 * deep, :wide]
        left = high[:, first:last]
        fields = jnp.concatenate([left, low[:, first:last], left], 1)
        return jnp.dot(fields, jnp.concatenate([top, top, rest], 0), preferred_element_type=F32)

    def inside(t, now, later):
        def stencil(cut):
            above, here = u[now, 0, :, cut], u[now, 1, :, cut]
            for a in range(1, na - 1):
                below = u[now, a + 1, :, cut]
                beside = shifted(here, 0.0, 0.0) + (above + below)
                value = ca[a, :, cut] * here + cc[a, :, cut] * beside + cb[a, :, cut]
                split(value, slice((a - 1) * nz, a * nz), cut, xh, xl)
                above, here = here, below

        ready = 0
        for place in places:
            start, stop, _, last, _ = place
            for l in range(ready, last, CHUNK):
                stencil(slice(l, l + CHUNK))
            ready = max(ready, last)
            total = solve(place, xh, xl).reshape(na - 2, nz, stop - start)
            active = jnp.full(total.shape, own_steps, jnp.int32) > t
            u[later, 1 : na - 1, :, start:stop] = jnp.where(active, total, u[now, 1 : na - 1, :, start:stop])

    def scatter(t, later, cut, face, near):
        for a in range(1, na - 1):
            u[later, a, face : face + 1, cut] = sz[t + 1, a : a + 1, cut]

    def border(t, now, later):
        def stencil(cut):
            for n, a, above, below in (
                (0, 0, ha[t, 0, :, cut], u[now, 1, :, cut]),
                (1, na - 1, u[now, na - 2, :, cut], ha[t, 1, :, cut]),
            ):
                here = u[now, a, :, cut]
                outer = hz[t, a : a + 1, cut]
                before, after = jnp.where(ax == 0, 0.0, outer), jnp.where(ax == 0, outer, 0.0)
                beside = shifted(here, before, after) + (above + below)
                value = ca[a, :, cut] * here + cc[a, :, cut] * beside + cb[a, :, cut]
                split(value, slice(n * nz, (n + 1) * nz), cut, bh, bl)
            before, after = (
                jnp.where(ax == 0, ha[t, side, nz - 1 : nz, cut], ha[t, side, 0:1, cut]) for side in (0, 1)
            )
            here = sz[t, :, cut]
            beside = shifted(here, before, after) + (inner[:, cut] + hz[t, :, cut])
            value = fa[:, cut] * here + fc[:, cut] * beside + fb[:, cut]
            split(value, slice(2 * nz, 2 * nz + na), cut, bh, bl)

        ready, arrived = 0, 0
        for place in places:
            start, stop, _, last, _ = place
            cut = slice(start, stop)
            while arrived < len(groups) and groups[arrived][0] < last:
                wait_halo(t, arrived)
                arrived += 1
            for l in range(ready, last, CHUNK):
                stencil(slice(l, l + CHUNK))
            ready = max(ready, last)
            total = solve(place, bh, bl)
            old = jnp.concatenate([u[now, 0, :, cut], u[now, na - 1, :, cut], sz[t, :, cut]], 0)
            total = jnp.where(jnp.full(total.shape, own_steps, jnp.int32) > t, total, old)
            u[later, 0, :, cut] = total[:nz]
            u[later, na - 1, :, cut] = total[nz : 2 * nz]
            sa[t + 1, 1, :, cut] = total[:nz]
            sa[t + 1, 0, :, cut] = total[nz : 2 * nz]
            sz[t + 1, :, cut] = total[2 * nz :]

            @pl.when(t < STEPS - 1)
            def _():
                for group, (begin, _) in enumerate(groups):
                    if start <= begin < stop:
                        send_halo(t + 1, group)

            @pl.when(t == STEPS - 1)
            def _():
                by_side(functools.partial(scatter, t, later, cut))
                loop(offsets, start // CHUNK, stop // CHUNK)

    def fine(t, _):
        now, later = lax.rem(t, 2), lax.rem(t + 1, 2)
        inside(t, now, later)
        border(t, now, later)

        def ready(face, near):
            scatter(t, later, slice(None), face, near)
            gather(u.at[later], near, inner)

        @pl.when(t < STEPS - 1)
        def _():
            by_side(ready)

        @pl.when(t == 0)
        def _():
            lax.fori_loop(0, half, own_factor, 0)
            lax.fori_loop(0, part, factors, 0)

        return 0

    by_side(lambda face, near: gather(u.at[0], near, inner))
    lax.fori_loop(0, STEPS, fine, 0)

    def pairs(k):
        mate_copy(k).wait_recv()
        cut = lanes_of(k)
        own, theirs = off[ours, :, cut], other[:, :, cut]
        even = jnp.where(core == 0, own, theirs)
        odd = jnp.where(core == 0, theirs, own)
        pair[:, :, cut] = fo[:, :, cut] * even + odd

    def forward(k):
        cut = lanes_of(k)

        @pl.when(chip > 0)
        def _():
            forward_copy(k).wait_recv()

        pout[:, :, cut] = fe[:, :, cut] * fo[:, :, cut] * pin[:, :, cut] + pair[:, :, cut]

        @pl.when(chip < chips - 1)
        def _():
            forward_copy(k).start()

    def backward(k):
        cut = lanes_of(k)

        @pl.when(chip < chips - 1)
        def _():
            backward_copy(k).wait_recv()

        sout[:, :, cut] = fs[:, :, cut] * pair[:, :, cut] + sin[:, :, cut]

        @pl.when(chip > 0)
        def _():
            backward_copy(k).start()

    def settle(k):
        cut = lanes_of(k)
        own, theirs = off[ours, :, cut], other[:, :, cut]
        first = jnp.where(core == 0, own, theirs)
        even = (fp[:, :, cut] * sout[:, :, cut] + pin[:, :, cut]) * inv[:, :, cut]
        odd = fe[:, :, cut] * even + first
        mine[:, :, cut] = jnp.where(core == 0, even, odd)
        give[:, :, cut] = jnp.where(core == 0, odd, even)
        coarse_copy(k).start()
        keep_copy(k).start()

    def send_change(k):
        change_copy(k).start()

    def both(first, second):
        def one(k):
            pairs(k)
            first(k)

            @pl.when(last_odd)
            def _():
                loop(send_change, due(k), due(k + 1))

        def relay(k):
            first(k)

            @pl.when(near_odd & (k + AHEAD < chunks))
            def _():
                send_change(k + AHEAD)

        def two(k):
            second(k)
            settle(k)

        @pl.when(ends)
        def _():
            loop(one)

            @pl.when((chip == 0) & (core == 1))
            def _():
                loop(send_change)

            @pl.when(last_odd)
            def _():
                loop(send_change, due(chunks), chunks)

            loop(two)

        @pl.when(jnp.logical_not(ends))
        def _():
            loop(pairs)
            loop(relay, 0, LAG)

            def step(k):
                relay(k)
                two(k - LAG)

            loop(step, LAG, chunks)
            loop(two, chunks - LAG, chunks)

    @pl.when(chip < chips // 2)
    def _():
        both(forward, backward)

    @pl.when(chip >= chips // 2)
    def _():
        both(backward, forward)

    keep_copy(None).wait()
    coarse_copy(None).wait()
    change_copy(None).wait()
    mate_copy(None).wait_send()

    @pl.when(chip < chips - 1)
    def _():
        forward_copy(None).wait_send()

    @pl.when(chip > 0)
    def _():
        backward_copy(None).wait_send()


def spread(coarse_ref, change_ref, out_ref):
    for r in range(coarse_ref.shape[0]):
        out_ref[0, 2 * r] = coarse_ref[r] + change_ref[r]
        out_ref[0, 2 * r + 1] = coarse_ref[r] - change_ref[r]


def solution(mesh):
    sizes = tuple(mesh.shape[name] for name in ("tm", "ang", "ax"))

    def local(starts, drive, region_ids, steps, reluctivity, resistivity, rates):
        na, nz, rad = region_ids.shape
        half, part = na // 2, na // 4
        blocks, places = inverse_blocks(rad)
        weights = np.concatenate(
            [np.pad(piece, ((0, 0), (0, WIDE - piece.shape[1]))) for block in blocks for piece in block]
        )
        smem = pl.BlockSpec(memory_space=pltpu.SMEM)
        anywhere = pl.BlockSpec(memory_space=pltpu.HBM)

        def field(*lead):
            return pltpu.VMEM(lead + (nz, rad), F32)

        halo = pltpu.VMEM((STEPS, 2, nz, rad), F32)
        face = pltpu.VMEM((STEPS, na, rad), F32)
        dma = pltpu.SemaphoreType.DMA
        edge = pltpu.VMEM((na, rad), F32)
        inside = pltpu.VMEM(((na - 2) * nz, rad), BF16)
        border = pltpu.VMEM((2 * nz + na, rad), BF16)
        scratch = [
            field(na), pltpu.VMEM((na, nz, rad), jnp.int32),
            field(2, na), field(na), field(na), field(na), field(half),
            inside, inside, border, border,
            halo, face, pltpu.VMEM((STEPS + 1, 2, nz, rad), F32), pltpu.VMEM((STEPS + 1, na, rad), F32), edge, edge, edge, edge,
            field(half), field(half), field(half), field(part),
        ]
        scratch += [field(part)] * 5 + [field(part)] * 7
        count = len(send_groups(places))
        scratch += [dma((2, count, 1 if sizes[1] == 2 else 2))] * 2 + [dma((2, count))] * 2 + [dma((1,)), dma((rad // CHUNK,)), dma((1,)), dma((1,))]
        scratch += [dma((1,)), dma((rad // CHUNK,))] * 2 + [dma((1,))] * 2
        scratch += [dma((4,)), dma((1,))]
        scratch += [pltpu.VMEM(weights.shape, BF16)]
        pairs = jax.ShapeDtypeStruct((half, nz, rad), F32)
        coarse, change = pl.pallas_call(
            functools.partial(kernel, sizes, places, [top.shape[0] for top, _ in blocks]),
            out_shape=(pairs, pairs),
            in_specs=[smem] * 4 + [anywhere] * 4,
            out_specs=[pl.BlockSpec(memory_space=pl.ANY)] * 2,
            scratch_shapes=scratch,
            compiler_params=pltpu.CompilerParams(
                collective_id=0, has_side_effects=True, vmem_limit_bytes=VMEM_LIMIT
            ),
        )(steps, reluctivity, resistivity, rates, starts, drive, region_ids, jnp.asarray(weights))
        rows = half // SPLIT
        narrow = pl.BlockSpec((rows, nz, rad), lambda i: (i, 0, 0))
        return pl.pallas_call(
            spread,
            grid=(SPLIT,),
            out_shape=jax.ShapeDtypeStruct(starts.shape, F32),
            in_specs=[narrow] * 2,
            out_specs=pl.BlockSpec((1, 2 * rows, nz, rad), lambda i: (0, i, 0, 0)),
        )(coarse, change)

    cells = P("tm", "ang", "ax", None)
    placed = (cells, cells, P("ang", "ax", None), P(), P(), P(), P())
    return jax.shard_map(local, mesh=mesh, in_specs=placed, out_specs=cells, check_vma=False)
```

```python
import functools

import jax
import jax.numpy as jnp
import ml_dtypes
import numpy as np
from jax import lax
from jax.experimental import pallas as pl
from jax.experimental.pallas import tpu as pltpu
from jax.sharding import PartitionSpec as P

STEPS = 4
LANES = 384
WIDE = 256
EDGE = 128
CHUNK = 128
TALL = 8
SPLIT = 2
VMEM_LIMIT = 60 * 2**20
AHEAD = 5
LAG = 5
BURST = 6
RATE = (1, 2)
FRONT = ()

radial_weight = 1.0
explicit_limit = 0.23
F32 = jnp.float32
BF16 = jnp.bfloat16


def inverse_blocks(size):
    middle = 2.0 + 1.0 / radial_weight
    r = (middle - np.sqrt(middle * middle - 4.0)) / 2.0
    index = np.arange(size, dtype=np.float64)
    low = np.minimum(index[:, None], index[None, :])
    high = np.maximum(index[:, None], index[None, :])
    full = r ** (high - low) * (1 - r ** (2 * low + 2)) * (1 - r ** (2 * (size - high)))
    full = full / ((1 / r - r) * (1 - r ** (2 * size + 2)) * radial_weight)
    full = full.astype(np.float32)
    blocks, places, seen = [], [], {}
    starts = [0, *range(size % WIDE or WIDE, size, WIDE)]
    for start, stop in zip(starts, starts[1:] + [size]):
        first, last = max(start - EDGE, 0), min(stop + EDGE, size)
        block = np.ascontiguousarray(full[first:last, start:stop])
        key = (block.shape, block.tobytes())
        if key not in seen:
            seen[key] = len(blocks)
            top = block.astype(ml_dtypes.bfloat16)
            rest = (block - top.astype(np.float32)).astype(ml_dtypes.bfloat16)
            blocks.append((top, rest))
        places.append((start, stop, first, last, seen[key]))
    return blocks, places


def send_groups(places):
    cuts = sorted({0, *FRONT, *(stop for _, stop, *_ in places)})
    return list(zip(cuts, cuts[1:]))


def kernel(sizes, places, depths, *refs):
    nblocks = len(depths)
    tm_count, ang_count, ax_count = sizes
    steps_ref, reluct_ref, resist_ref, rates_ref, s_hbm, q_hbm, ids_hbm = refs[:7]
    w_hbm, coarse_ref, rdif = refs[7:10]
    (
        q_ref, ids_ref, u, ca, cc, cb, rc, xh, xl, bh, bl, ha, hz, sa, sz, inner, fa, fc, fb,
        gs, off, dif, other, fs, fp, inv, fe, fo,
        pair, pin, sin, pout, sout, mine, give,
        a_send, a_recv, z_send, z_recv, o_send, o_recv,
        d_send, d_recv, p_send, p_recv, q_send, q_recv, c_send, c_recv, in_sem, out_sem, w_all
    ) = refs[10:]
    na, nz, rad = ids_ref.shape
    wedges = dict(zip(range(nblocks), np.cumsum([0, *depths])))
    half = na // 2
    part = half // 2
    regions = rates_ref.shape[0]
    tm, ang, ax = lax.axis_index("tm"), lax.axis_index("ang"), lax.axis_index("ax")
    core, chip = lax.rem(tm, 2), tm // 2
    chips = tm_count // 2
    mate = tm + 1 - 2 * core

    def ring(value, step, count):
        return lax.rem(value + step + count, count)

    loads = [(s_hbm.at[0], u.at[0]), (ids_hbm, ids_ref), (q_hbm.at[0], q_ref), (w_hbm, w_all)]
    loads = [pltpu.make_async_copy(a, b, in_sem.at[n]) for n, (a, b) in enumerate(loads)]
    barrier = pltpu.get_barrier_semaphore()
    greet = [("ang", ang, step, ang_count) for step in ((1,) if ang_count == 2 else (1, -1))]
    greet += [("ax", ax, 1, ax_count)]
    greet += [("tm", tm, step, tm_count) for step in (1, -1, 2, -2)]
    for axis, value, step, count in greet:
        pl.semaphore_signal(
            barrier, inc=1, device_id={axis: ring(value, step, count)},
            device_id_type=pl.DeviceIdType.MESH,
        )

    for load in loads:
        load.start()

    def remote(src, dst, send, recv, device):
        return pltpu.make_async_remote_copy(
            src_ref=src, dst_ref=dst, send_sem=send, recv_sem=recv,
            device_id=device, device_id_type=pl.DeviceIdType.MESH,
        )

    groups = send_groups(places)

    def ang_copies(t, block):
        lanes = slice(*groups[block])
        if ang_count == 2:
            routes = [(slice(None), 1 - ang)]
        else:
            routes = [(0, ring(ang, 1, ang_count)), (1, ring(ang, -1, ang_count))]
        return [
            remote(
                sa.at[t, side, :, lanes], ha.at[t, side, :, lanes],
                a_send.at[lax.rem(t, 2), block, n], a_recv.at[lax.rem(t, 2), block, n], {"ang": device},
            )
            for n, (side, device) in enumerate(routes)
        ]

    def ax_copy(t, block):
        lanes = slice(*groups[block])
        return remote(
            sz.at[t, :, lanes], hz.at[t, :, lanes],
            z_send.at[lax.rem(t, 2), block], z_recv.at[lax.rem(t, 2), block], {"ax": 1 - ax},
        )

    def send_halo(t, block):
        ax_copy(t, block).start()
        for copy in ang_copies(t, block):
            copy.start()

    def wait_halo(t, block):
        for copy in ang_copies(t, block):
            copy.wait()
        ax_copy(t, block).wait()

    def by_side(body):
        @pl.when(ax == 0)
        def _():
            body(nz - 1, nz - 2)

        @pl.when(ax == 1)
        def _():
            body(0, 1)

    def gather(field, face, into):
        for a in range(na):
            into[a : a + 1, :] = field[a, face : face + 1, :]

    loads[0].wait()
    sa[0, 0] = u[0, na - 1]
    sa[0, 1] = u[0, 0]
    pl.semaphore_wait(barrier, len(greet))
    for block in range(len(groups)):
        for copy in ang_copies(0, block):
            copy.start()
    by_side(lambda face, near: gather(u.at[0], face, sz.at[0]))
    for block in range(len(groups)):
        ax_copy(0, block).start()

    @pl.when(chip == 0)
    def _():
        pin[...] = jnp.zeros_like(pin)

    @pl.when(chip == chips - 1)
    def _():
        sin[...] = jnp.zeros_like(sin)

    loads[1].wait()
    loads[2].wait()
    reluct = [explicit_limit * reluct_ref[k] * resist_ref[k] for k in range(regions)]
    rates = [rates_ref[k] for k in range(regions)]
    own_steps = steps_ref[tm]

    def tables(a, _):
        for l in range(0, rad, LANES):
            cut = slice(l, l + LANES)
            ids = ids_ref[a, :, cut]
            coupling = jnp.zeros(ids.shape, F32)
            relax = jnp.zeros(ids.shape, F32)
            for k in range(regions):
                hit = ids == k
                coupling = jnp.where(hit, reluct[k], coupling)
                relax = jnp.where(hit, rates[k], relax)
            cc[a, :, cut] = coupling
            ca[a, :, cut] = 1.0 - 4.0 * coupling - relax
            cb[a, :, cut] = relax * q_ref[a, :, cut]
            previous = rc[a // 2, :, cut]
            rc[a // 2, :, cut] = jnp.where(lax.rem(a, 2) == 0, relax, 0.5 * (previous + relax))
        return 0

    lax.fori_loop(0, na, tables, 0)

    def side_tables(face, near):
        for field, into in ((ca, fa), (cc, fc), (cb, fb)):
            gather(field, face, into)

    by_side(side_tables)

    def own_factor(i, _):
        mean = (u[0, 2 * i] + u[0, 2 * i + 1]) * 0.5
        gs[i] = mean / (1.0 + own_steps.astype(F32) * rc[i])
        return 0


    def factors(k, _):
        rate = rc[part * core + k]
        before = jnp.ones_like(rate)
        after = jnp.ones_like(rate)
        for j in range(tm_count):
            count = steps_ref[j].astype(F32)
            before = before * (1.0 + jnp.where(j < 2 * chip, count, 0.0) * rate)
            after = after * (1.0 + jnp.where(j > 2 * chip + 1, count, 0.0) * rate)
        even = 1.0 + steps_ref[2 * chip].astype(F32) * rate
        odd = 1.0 + steps_ref[2 * chip + 1].astype(F32) * rate
        whole = before * after * (even * odd)
        fs[k] = 1.0 / after
        fp[k] = 1.0 / before
        fe[k] = 1.0 / even
        fo[k] = 1.0 / odd
        inv[k] = whole / (whole - 1.0)
        return 0

    for load in loads[3:]:
        load.wait()

    chunks = rad // CHUNK

    def lanes_of(k):
        if k is None:
            return slice(None)
        return pl.ds(pl.multiple_of(k * CHUNK, CHUNK), CHUNK)

    ours, yours = pl.ds(part * core, part), pl.ds(part * (1 - core), part)

    def mate_copy(k):
        cut = lanes_of(k)
        return remote(
            off.at[yours, :, cut], other.at[:, :, cut], o_send.at[0], o_recv.at[0 if k is None else k], {"tm": mate}
        )

    def change_copy(k):
        cut = lanes_of(k)
        return remote(
            dif.at[:, :, cut], rdif.at[:, :, cut], d_send.at[0], d_recv.at[0],
            {"tm": ring(tm, 1, tm_count)},
        )

    def forward_copy(k):
        cut = lanes_of(k)
        return remote(
            pout.at[:, :, cut], pin.at[:, :, cut], p_send.at[0], p_recv.at[0 if k is None else k],
            {"tm": ring(tm, 2, tm_count)},
        )

    def backward_copy(k):
        cut = lanes_of(k)
        return remote(
            sout.at[:, :, cut], sin.at[:, :, cut], q_send.at[0], q_recv.at[0 if k is None else k],
            {"tm": ring(tm, -2, tm_count)},
        )

    def coarse_copy(k):
        cut = lanes_of(k)
        return remote(
            give.at[:, :, cut], coarse_ref.at[ours, :, cut], c_send.at[0], c_recv.at[0], {"tm": mate}
        )

    def keep_copy(k):
        cut = lanes_of(k)
        return pltpu.make_async_copy(mine.at[:, :, cut], coarse_ref.at[ours, :, cut], out_sem.at[0])

    def loop(body, first=0, last=chunks):
        def step(k, _):
            body(k)
            return 0

        lax.fori_loop(first, last, step, 0)

    ends = (chip == 0) | (chip == chips - 1)
    near_odd = jnp.logical_not(ends) & (core == 1)
    last_odd = (chip == chips - 1) & (core == 1)

    def due(k):
        return jnp.minimum(BURST + k * RATE[0] // RATE[1], chunks)

    def offsets(k):
        cut = lanes_of(k)
        for i in range(half):
            even, odd = u[STEPS % 2, 2 * i, :, cut], u[STEPS % 2, 2 * i + 1, :, cut]
            off[i, :, cut] = (even + odd) * 0.5 - gs[i, :, cut]
            dif[i, :, cut] = (even - odd) * 0.5
        mate_copy(k).start()

        soon = (core == 0) | (near_odd & (k < AHEAD)) | (last_odd & (k < BURST))

        @pl.when(soon)
        def _():
            change_copy(k).start()

    spot = lax.broadcasted_iota(jnp.int32, (TALL, CHUNK), 0)
    low_edge, high_edge = spot == 0, spot == TALL - 1

    def shifted(here, before, after):
        pieces = [here[r : r + TALL] for r in range(0, here.shape[0], TALL)]
        down = [before] + [pltpu.roll(piece, 1, 0) for piece in pieces]
        up = [pltpu.roll(piece, TALL - 1, 0) for piece in pieces] + [after]
        both = [
            jnp.where(low_edge, down[r], down[r + 1]) + jnp.where(high_edge, up[r + 1], up[r])
            for r in range(len(pieces))
        ]
        return jnp.concatenate(both, 0)

    def split(value, rows, cut, high, low):
        top = value.astype(BF16)
        high[rows, cut] = top
        low[rows, cut] = (value - top.astype(F32)).astype(BF16)

    def solve(place, high, low):
        start, stop, first, last, which = place
        row, deep, wide = 2 * wedges[which], last - first, stop - start
        top, rest = w_all[row : row + deep, :wide], w_all[row + deep : row + 2 * deep, :wide]
        left = high[:, first:last]
        fields = jnp.concatenate([left, low[:, first:last], left], 1)
        return jnp.dot(fields, jnp.concatenate([top, top, rest], 0), preferred_element_type=F32)

    def inside(t, now, later):
        def stencil(cut):
            above, here = u[now, 0, :, cut], u[now, 1, :, cut]
            for a in range(1, na - 1):
                below = u[now, a + 1, :, cut]
                beside = shifted(here, 0.0, 0.0) + (above + below)
                value = ca[a, :, cut] * here + cc[a, :, cut] * beside + cb[a, :, cut]
                split(value, slice((a - 1) * nz, a * nz), cut, xh, xl)
                above, here = here, below

        ready = 0
        for place in places:
            start, stop, _, last, _ = place
            for l in range(ready, last, CHUNK):
                stencil(slice(l, l + CHUNK))
            ready = max(ready, last)
            total = solve(place, xh, xl).reshape(na - 2, nz, stop - start)
            active = jnp.full(total.shape, own_steps, jnp.int32) > t
            u[later, 1 : na - 1, :, start:stop] = jnp.where(active, total, u[now, 1 : na - 1, :, start:stop])

    def scatter(t, later, cut, face, near):
        for a in range(1, na - 1):
            u[later, a, face : face + 1, cut] = sz[t + 1, a : a + 1, cut]

    def border(t, now, later):
        def stencil(cut):
            for n, a, above, below in (
                (0, 0, ha[t, 0, :, cut], u[now, 1, :, cut]),
                (1, na - 1, u[now, na - 2, :, cut], ha[t, 1, :, cut]),
            ):
                here = u[now, a, :, cut]
                outer = hz[t, a : a + 1, cut]
                before, after = jnp.where(ax == 0, 0.0, outer), jnp.where(ax == 0, outer, 0.0)
                beside = shifted(here, before, after) + (above + below)
                value = ca[a, :, cut] * here + cc[a, :, cut] * beside + cb[a, :, cut]
                split(value, slice(n * nz, (n + 1) * nz), cut, bh, bl)
            before, after = (
                jnp.where(ax == 0, ha[t, side, nz - 1 : nz, cut], ha[t, side, 0:1, cut]) for side in (0, 1)
            )
            here = sz[t, :, cut]
            beside = shifted(here, before, after) + (inner[:, cut] + hz[t, :, cut])
            value = fa[:, cut] * here + fc[:, cut] * beside + fb[:, cut]
            split(value, slice(2 * nz, 2 * nz + na), cut, bh, bl)

        ready, arrived = 0, 0
        for place in places:
            start, stop, _, last, _ = place
            cut = slice(start, stop)
            while arrived < len(groups) and groups[arrived][0] < last:
                wait_halo(t, arrived)
                arrived += 1
            for l in range(ready, last, CHUNK):
                stencil(slice(l, l + CHUNK))
            ready = max(ready, last)
            total = solve(place, bh, bl)
            old = jnp.concatenate([u[now, 0, :, cut], u[now, na - 1, :, cut], sz[t, :, cut]], 0)
            total = jnp.where(jnp.full(total.shape, own_steps, jnp.int32) > t, total, old)
            u[later, 0, :, cut] = total[:nz]
            u[later, na - 1, :, cut] = total[nz : 2 * nz]
            sa[t + 1, 1, :, cut] = total[:nz]
            sa[t + 1, 0, :, cut] = total[nz : 2 * nz]
            sz[t + 1, :, cut] = total[2 * nz :]

            @pl.when(t < STEPS - 1)
            def _():
                for group, (begin, _) in enumerate(groups):
                    if start <= begin < stop:
                        send_halo(t + 1, group)

            @pl.when(t == STEPS - 1)
            def _():
                by_side(functools.partial(scatter, t, later, cut))
                loop(offsets, start // CHUNK, stop // CHUNK)

    def fine(t, _):
        now, later = lax.rem(t, 2), lax.rem(t + 1, 2)
        inside(t, now, later)
        border(t, now, later)

        def ready(face, near):
            scatter(t, later, slice(None), face, near)
            gather(u.at[later], near, inner)

        @pl.when(t < STEPS - 1)
        def _():
            by_side(ready)

        @pl.when(t == 0)
        def _():
            lax.fori_loop(0, half, own_factor, 0)
            lax.fori_loop(0, part, factors, 0)

        return 0

    by_side(lambda face, near: gather(u.at[0], near, inner))
    lax.fori_loop(0, STEPS, fine, 0)

    def pairs(k):
        mate_copy(k).wait_recv()
        cut = lanes_of(k)
        own, theirs = off[ours, :, cut], other[:, :, cut]
        even = jnp.where(core == 0, own, theirs)
        odd = jnp.where(core == 0, theirs, own)
        pair[:, :, cut] = fo[:, :, cut] * even + odd

    def forward(k):
        cut = lanes_of(k)

        @pl.when(chip > 0)
        def _():
            forward_copy(k).wait_recv()

        pout[:, :, cut] = fe[:, :, cut] * fo[:, :, cut] * pin[:, :, cut] + pair[:, :, cut]

        @pl.when(chip < chips - 1)
        def _():
            forward_copy(k).start()

    def backward(k):
        cut = lanes_of(k)

        @pl.when(chip < chips - 1)
        def _():
            backward_copy(k).wait_recv()

        sout[:, :, cut] = fs[:, :, cut] * pair[:, :, cut] + sin[:, :, cut]

        @pl.when(chip > 0)
        def _():
            backward_copy(k).start()

    def settle(k):
        cut = lanes_of(k)
        own, theirs = off[ours, :, cut], other[:, :, cut]
        first = jnp.where(core == 0, own, theirs)
        even = (fp[:, :, cut] * sout[:, :, cut] + pin[:, :, cut]) * inv[:, :, cut]
        odd = fe[:, :, cut] * even + first
        mine[:, :, cut] = jnp.where(core == 0, even, odd)
        give[:, :, cut] = jnp.where(core == 0, odd, even)
        coarse_copy(k).start()
        keep_copy(k).start()

    def send_change(k):
        change_copy(k).start()

    def both(first, second):
        def one(k):
            pairs(k)
            first(k)

            @pl.when(last_odd)
            def _():
                loop(send_change, due(k), due(k + 1))

        def relay(k):
            first(k)

            @pl.when(near_odd & (k + AHEAD < chunks))
            def _():
                send_change(k + AHEAD)

        def two(k):
            second(k)
            settle(k)

        @pl.when(ends)
        def _():
            loop(one)

            @pl.when((chip == 0) & (core == 1))
            def _():
                loop(send_change)

            @pl.when(last_odd)
            def _():
                loop(send_change, due(chunks), chunks)

            loop(two)

        @pl.when(jnp.logical_not(ends))
        def _():
            loop(pairs)
            loop(relay, 0, LAG)

            def step(k):
                relay(k)
                two(k - LAG)

            loop(step, LAG, chunks)
            loop(two, chunks - LAG, chunks)

    @pl.when(chip < chips // 2)
    def _():
        both(forward, backward)

    @pl.when(chip >= chips // 2)
    def _():
        both(backward, forward)

    keep_copy(None).wait()
    coarse_copy(None).wait()
    change_copy(None).wait()
    mate_copy(None).wait_send()

    @pl.when(chip < chips - 1)
    def _():
        forward_copy(None).wait_send()

    @pl.when(chip > 0)
    def _():
        backward_copy(None).wait_send()


def spread(coarse_ref, change_ref, out_ref):
    for r in range(coarse_ref.shape[0]):
        out_ref[0, 2 * r] = coarse_ref[r] + change_ref[r]
        out_ref[0, 2 * r + 1] = coarse_ref[r] - change_ref[r]


def solution(mesh):
    sizes = tuple(mesh.shape[name] for name in ("tm", "ang", "ax"))

    def local(starts, drive, region_ids, steps, reluctivity, resistivity, rates):
        na, nz, rad = region_ids.shape
        half, part = na // 2, na // 4
        blocks, places = inverse_blocks(rad)
        weights = np.concatenate(
            [np.pad(piece, ((0, 0), (0, WIDE - piece.shape[1]))) for block in blocks for piece in block]
        )
        smem = pl.BlockSpec(memory_space=pltpu.SMEM)
        anywhere = pl.BlockSpec(memory_space=pltpu.HBM)

        def field(*lead):
            return pltpu.VMEM(lead + (nz, rad), F32)

        halo = pltpu.VMEM((STEPS, 2, nz, rad), F32)
        face = pltpu.VMEM((STEPS, na, rad), F32)
        dma = pltpu.SemaphoreType.DMA
        edge = pltpu.VMEM((na, rad), F32)
        inside = pltpu.VMEM(((na - 2) * nz, rad), BF16)
        border = pltpu.VMEM((2 * nz + na, rad), BF16)
        scratch = [
            field(na), pltpu.VMEM((na, nz, rad), jnp.int32),
            field(2, na), field(na), field(na), field(na), field(half),
            inside, inside, border, border,
            halo, face, pltpu.VMEM((STEPS + 1, 2, nz, rad), F32), pltpu.VMEM((STEPS + 1, na, rad), F32), edge, edge, edge, edge,
            field(half), field(half), field(half), field(part),
        ]
        scratch += [field(part)] * 5 + [field(part)] * 7
        count = len(send_groups(places))
        scratch += [dma((2, count, 1 if sizes[1] == 2 else 2))] * 2 + [dma((2, count))] * 2 + [dma((1,)), dma((rad // CHUNK,)), dma((1,)), dma((1,))]
        scratch += [dma((1,)), dma((rad // CHUNK,))] * 2 + [dma((1,))] * 2
        scratch += [dma((4,)), dma((1,))]
        scratch += [pltpu.VMEM(weights.shape, BF16)]
        pairs = jax.ShapeDtypeStruct((half, nz, rad), F32)
        coarse, change = pl.pallas_call(
            functools.partial(kernel, sizes, places, [top.shape[0] for top, _ in blocks]),
            out_shape=(pairs, pairs),
            in_specs=[smem] * 4 + [anywhere] * 4,
            out_specs=[pl.BlockSpec(memory_space=pl.ANY)] * 2,
            scratch_shapes=scratch,
            compiler_params=pltpu.CompilerParams(
                collective_id=0, has_side_effects=True, vmem_limit_bytes=VMEM_LIMIT
            ),
        )(steps, reluctivity, resistivity, rates, starts, drive, region_ids, jnp.asarray(weights))
        rows = half // SPLIT
        narrow = pl.BlockSpec((rows, nz, rad), lambda i: (i, 0, 0))
        return pl.pallas_call(
            spread,
            grid=(SPLIT,),
            out_shape=jax.ShapeDtypeStruct(starts.shape, F32),
            in_specs=[narrow] * 2,
            out_specs=pl.BlockSpec((1, 2 * rows, nz, rad), lambda i: (0, i, 0, 0)),
        )(coarse, change)

    cells = P("tm", "ang", "ax", None)
    placed = (cells, cells, P("ang", "ax", None), P(), P(), P(), P())
    return jax.shard_map(local, mesh=mesh, in_specs=placed, out_specs=cells, check_vma=False)
```
